128 devices in a mesh: dp: 2 (over z_lo), fsdp: 8 (over x, core), seq: 8 (over z_hi, y).
Axes of the slice: x: 4, y: 4, z: 4 (z_hi: 2, z_lo: 2; z = z_hi * 2 + z_lo), core: 2. Of those that a mesh axis runs over, the one named last changes fastest.
Arguments:
- tokens: bfloat16 [2, 32, 8, 8, 4096], P('dp', 'seq', None, None, 'fsdp'), may hold values from -6 to 6
- grad_out: bfloat16 [2, 32, 8, 8, 4096], P('dp', 'seq', None, None, 'fsdp'), may hold values from -6 to 6
- gain: float32 [4096], P('fsdp'), may hold values from 0.1 to 1.9
- up_weight: bfloat16 [4096, 8192], P('seq', 'fsdp'), may hold values from -0.09375 to 0.09375
- down_weight: bfloat16 [8192, 4096], P('fsdp', 'seq'), may hold values from -0.0625 to 0.0625
- conv_taps: float32 [27, 8192], P(None, 'fsdp'), may hold values from -1.25 to 1.25
Outputs:
- mixed: bfloat16 [2, 32, 8, 8, 4096], P('dp', 'seq', None, None, 'fsdp')
- grad_tokens: bfloat16 [2, 32, 8, 8, 4096], P('dp', 'seq', None, None, 'fsdp')
- grad_up: bfloat16 [4096, 8192], P('seq', 'fsdp')
- grad_down: bfloat16 [8192, 4096], P('fsdp', 'seq')
- grad_conv: float32 [27, 8192], P(None, 'fsdp')
- grad_gain: float32 [4096], P('fsdp')
The draws below stay inside these ranges and needn't reach their ends.
All inputs are finite; a program needn't handle non-finite values.
Results may differ from the reference program's by a relative error of at most 0.025.
Values may be sent and summed in bfloat16 or wider, within the bound.
A program may use at most 128 MiB of HBM per device.

```python
import jax
import jax.numpy as jnp
from jax import lax

D = 4096
FFW = 8192
GY = 8
GZ = 8
SNAPS = 2
NX = 32
N_DP = 2
N_FSDP = 8
N_SEQ = 8


def shard_levels(stream_key, shape, pieces, smallest, top_value):
    def one(position, blocks):
        heights = jax.random.uniform(jax.random.fold_in(jax.random.fold_in(stream_key, 6), position), (blocks,), jnp.float32, smallest / len(pieces), top_value / len(pieces))
        return jnp.repeat(jnp.exp(heights), shape[position] // blocks).reshape((-1,) + (1,) * (len(shape) - position - 1))

    loudness = one(*pieces[0])
    for cut in pieces[1:]:
        loudness = loudness * one(*cut)
    return loudness


def gaussian(own_key, shape, scale, limit, pieces=(), held_as=jnp.bfloat16):
    level = shard_levels(own_key, shape, pieces, -0.22, 0.18) if pieces else 1.0
    array = jax.random.normal(own_key, shape, jnp.float32) * scale * level
    return jnp.minimum(jnp.maximum(array, -limit), limit).astype(held_as)


def setup_inputs(seed: int = 0) -> dict:
    streams_of = jax.random.split(jax.random.key(seed), 7)
    return {
        "tokens": gaussian(streams_of[0], (SNAPS, NX, GY, GZ, D), 1.0, 6.0, ((0, 2), (1, 8), (4, 8))),
        "grad_out": gaussian(streams_of[1], (SNAPS, NX, GY, GZ, D), 1.0, 6.0, ((0, 2), (1, 8), (4, 8))),
        "gain": jnp.clip(1.0 + 0.18 * jax.random.normal(streams_of[2], (D,), jnp.float32), 0.1, 1.9),
        "up_weight": gaussian(streams_of[3], (D, FFW), D ** -0.5, 0.09375, ((0, 8), (1, 8))),
        "down_weight": gaussian(streams_of[4], (FFW, D), FFW ** -0.5, 0.0625, ((0, 8), (1, 8))),
        "conv_taps": gaussian(streams_of[5], (27, FFW), 27 ** -0.5, 1.25, ((1, 8),), jnp.float32),
    }


gelu_scale = 0.7978845608028654
gelu_cubic = 0.044715
epsilon = 1e-06

def gelu_pair(preact):
    inner = gelu_scale * (preact + gelu_cubic * preact * preact * preact)
    tangent = jnp.tanh(inner)
    value = 0.5 * preact * (1.0 + tangent)
    slope = 0.5 * (1.0 + tangent) + 0.5 * preact * (1.0 - tangent * tangent) * gelu_scale * (1.0 + 3.0 * gelu_cubic * preact * preact)
    return (value, slope)

def conv_apply(padded, kernel, flipped):
    planes = padded.shape[1] - 2
    side_y = padded.shape[2] - 2
    side_z = padded.shape[3] - 2
    total = jnp.zeros((padded.shape[0], planes, side_y, side_z, padded.shape[4]), jnp.float32)
    for shift_x in range(3):
        for shift_y in range(3):
            for shift_z in range(3):
                tap_row = kernel[shift_x * 9 + shift_y * 3 + shift_z]
                if flipped:
                    begin_x, begin_y, begin_z = (2 - shift_x, 2 - shift_y, 2 - shift_z)
                else:
                    begin_x, begin_y, begin_z = (shift_x, shift_y, shift_z)
                window = padded[:, begin_x:begin_x + planes, begin_y:begin_y + side_y, begin_z:begin_z + side_z, :]
                total = total + tap_row * window.astype(jnp.float32)
    return total

def conv_grad(d_grid, padded):
    planes, side_y, side_z = (d_grid.shape[1], d_grid.shape[2], d_grid.shape[3])
    d_float = d_grid.astype(jnp.float32)
    collected = []
    for shift_x in range(3):
        for shift_y in range(3):
            for shift_z in range(3):
                window = padded[:, shift_x:shift_x + planes, shift_y:shift_y + side_y, shift_z:shift_z + side_z, :]
                collected.append(lax.optimization_barrier(jnp.sum(d_float * window.astype(jnp.float32), axis=(0, 1, 2, 3))))
    return jnp.stack(collected)

def hidden_block_sum(left, right, blocks):
    size = left.shape[1] // blocks

    def step(index, total):
        start = (index * size).astype(jnp.int32)
        left_part = lax.dynamic_slice_in_dim(left, start, size, 1)
        right_part = lax.dynamic_slice_in_dim(right, start, size, 0)
        part = jnp.dot(left_part, right_part, preferred_element_type=jnp.float32).astype(jnp.bfloat16)
        part = lax.optimization_barrier(part)
        return total + part.astype(jnp.float32)
    return lax.fori_loop(0, blocks, step, jnp.zeros((left.shape[0], right.shape[1]), jnp.float32))

def token_block_sum(left, right, blocks):
    size = left.shape[0] // blocks

    def step(index, total):
        start = (index * size).astype(jnp.int32)
        left_part = lax.dynamic_slice_in_dim(left, start, size, 0)
        right_part = lax.dynamic_slice_in_dim(right, start, size, 0)
        part = lax.dot_general(left_part, right_part, (((0,), (0,)), ((), ())), preferred_element_type=jnp.float32).astype(jnp.bfloat16)
        part = lax.optimization_barrier(part)
        return total + part.astype(jnp.float32)
    return lax.fori_loop(0, blocks, step, jnp.zeros((left.shape[1], right.shape[1]), jnp.float32))

def reference(tokens, grad_out, gain, up_weight, down_weight, conv_taps):
    snaps, cells_x, side_y, side_z, width = tokens.shape
    hidden = up_weight.shape[1]
    rows = snaps * cells_x * side_y * side_z
    flat = tokens.reshape(rows, width).astype(jnp.float32)
    inverse = lax.rsqrt(lax.optimization_barrier(jnp.mean(flat * flat, axis=1, keepdims=True)) + epsilon)
    normed_hat = flat * inverse
    normed = (normed_hat * gain).astype(jnp.bfloat16)
    lifted = jnp.dot(normed, up_weight, preferred_element_type=jnp.float32).astype(jnp.bfloat16)
    grid = lifted.reshape(snaps, cells_x, side_y, side_z, hidden)
    padded = jnp.pad(grid, ((0, 0), (1, 1), (1, 1), (1, 1), (0, 0)))
    kernel = conv_taps.astype(jnp.float32)
    preact = conv_apply(padded, kernel, False)
    value, slope = gelu_pair(preact)
    active = value.astype(jnp.bfloat16).reshape(rows, hidden)
    branch = hidden_block_sum(active, down_weight, N_FSDP)
    mixed = (flat + branch).astype(jnp.bfloat16).reshape(tokens.shape)
    cot_flat = grad_out.reshape(rows, width)
    d_active = lax.dot_general(cot_flat, down_weight, (((1,), (1,)), ((), ())), preferred_element_type=jnp.float32)
    d_preact = (d_active * slope.reshape(rows, hidden)).astype(jnp.bfloat16)
    d_grid = d_preact.reshape(snaps, cells_x, side_y, side_z, hidden)
    d_padded = jnp.pad(d_grid, ((0, 0), (1, 1), (1, 1), (1, 1), (0, 0)))
    d_lifted = conv_apply(d_padded, kernel, True).astype(jnp.bfloat16).reshape(rows, hidden)
    grad_conv = conv_grad(d_grid, padded)
    blocks = N_DP * N_SEQ
    grad_up = token_block_sum(normed, d_lifted, blocks).astype(jnp.bfloat16)
    grad_down = token_block_sum(active, cot_flat, blocks).astype(jnp.bfloat16)
    d_norm = hidden_block_sum(d_lifted, up_weight.T, N_FSDP)
    d_hat = d_norm * gain
    row_total = lax.optimization_barrier(jnp.sum(d_hat * normed_hat, axis=1, keepdims=True))
    grad_tokens = (cot_flat.astype(jnp.float32) + inverse * (d_hat - normed_hat * row_total / width)).astype(jnp.bfloat16).reshape(tokens.shape)
    grad_gain = lax.optimization_barrier(jnp.sum(d_norm * normed_hat, axis=0))
    return (mixed, grad_tokens, grad_up, grad_down, grad_conv, grad_gain)
```

```python
import functools

import jax
import jax.numpy as jnp
from jax import lax
from jax.experimental import pallas as pl
from jax.experimental.pallas import tpu as pltpu
from jax.sharding import PartitionSpec as P

MESH = pl.DeviceIdType.MESH
gelu_scale = 0.7978845608028654
gelu_cubic = 0.044715
epsilon = 1e-06
B = 512


class Place:
    def __init__(self):
        self.zl = lax.axis_index("dp")
        self.f = lax.axis_index("fsdp")
        self.s = lax.axis_index("seq")
        self.x, self.c = lax.div(self.f, 2), lax.rem(self.f, 2)
        self.zh, self.y = lax.div(self.s, 4), lax.rem(self.s, 4)
        self.xs = [lax.rem(self.x + k, 4) for k in range(4)]
        self.ys = [lax.rem(self.y + k, 4) for k in range(4)]
        self.other_zl = {"dp": 1 - self.zl}
        self.other_core = {"fsdp": self.feat(0, 1)}
        self.x_up, self.x_down = {"fsdp": self.feat(1)}, {"fsdp": self.feat(3)}
        self.other_zh = {"seq": self.slab(0, 1)}
        self.y_up, self.y_down = {"seq": self.slab(1)}, {"seq": self.slab(3)}

    def feat(self, k, flip=0):
        return self.xs[k] * 2 + (1 - self.c if flip else self.c)

    def slab(self, k, flip=0):
        return (1 - self.zh if flip else self.zh) * 4 + self.ys[k]

    def partners(self):
        return [self.other_zl, self.other_core, self.x_up, self.x_down, self.other_zh, self.y_up, self.y_down]


class Wires:
    def __init__(self, send, recv):
        self.send, self.recv, self.copies = send, recv, []

    def start(self, src, dst, where):
        i = len(self.copies)
        copy = pltpu.make_async_remote_copy(
            src_ref=src, dst_ref=dst, send_sem=self.send.at[i], recv_sem=self.recv.at[i],
            device_id=where, device_id_type=MESH,
        )
        copy.start()
        self.copies.append(copy)
        return copy

    def finish(self):
        for copy in self.copies:
            copy.wait_send()


def meet(partners):
    barrier = pltpu.get_barrier_semaphore()
    for where in partners:
        pl.semaphore_signal(barrier, inc=1, device_id=where, device_id_type=MESH)
    pl.semaphore_wait(barrier, len(partners))


class WeightGather:
    def __init__(self, me, wires, own, buf):
        self.me, self.wires, self.own, self.buf = me, wires, own, buf

    def start_z(self):
        self.z = self.wires.start(self.own, self.buf.at[self.me.s], self.me.other_zh)

    def start_y(self):
        self.up = self.wires.start(self.own, self.buf.at[self.me.s], self.me.y_up)
        self.down = self.wires.start(self.own, self.buf.at[self.me.s], self.me.y_down)

    def forward(self, flip):
        me, buf = self.me, self.buf
        below, above = me.slab(3, flip), me.slab(1, flip)
        self.up.wait_recv()
        part = buf.at[below, pl.ds(0, B // 2)]
        first = self.wires.start(part, part, me.y_up)
        self.down.wait_recv()
        part = buf.at[above, pl.ds(B // 2, B // 2)]
        return first, self.wires.start(part, part, me.y_down)

    def forward_own(self):
        self.far = self.forward(0)

    def start_other(self):
        self.z.wait_recv()
        block = self.buf.at[self.me.slab(0, 1)]
        self.up = self.wires.start(block, block, self.me.y_up)
        self.down = self.wires.start(block, block, self.me.y_down)

    def forward_other(self):
        self.far_other = self.forward(1)

    def wait_far(self):
        for copy in self.far:
            copy.wait_recv()

    def wait_far_other(self):
        for copy in self.far_other:
            copy.wait_recv()


class TokenGather:
    def __init__(self, me, wires, own, buf):
        self.me, self.wires, self.own, self.buf = me, wires, own, buf
        self.cores = []

    def rows(self, half, part=None):
        if part is None:
            return pl.ds(pl.multiple_of(half * 256, 256), 256)
        return pl.ds(pl.multiple_of(half * 256 + part * 128, 128), 128)

    def start_own(self):
        me = self.me
        dst = self.buf.at[me.f, self.rows(me.zl)]
        self.z = self.wires.start(self.own, dst, me.other_zl)
        self.ring = [self.wires.start(self.own, dst, where) for where in (me.x_up, me.x_down)]
        self.cores.append(self.wires.start(self.own, dst, me.other_core))

    def to_core(self, k, half):
        block = self.buf.at[self.me.feat(k), self.rows(half)]
        self.cores.append(self.wires.start(block, block, self.me.other_core))

    def forward(self, half):
        me, buf, ring = self.me, self.buf, self.ring
        ring[0].wait_recv()
        part = buf.at[me.feat(3), self.rows(half, 0)]
        first = self.wires.start(part, part, me.x_up)
        ring[1].wait_recv()
        part = buf.at[me.feat(1), self.rows(half, 1)]
        self.far = first, self.wires.start(part, part, me.x_down)
        self.to_core(3, half)
        self.to_core(1, half)

    def start_other(self):
        me = self.me
        self.z.wait_recv()
        block = self.buf.at[me.f, self.rows(1 - me.zl)]
        self.ring = [self.wires.start(block, block, where) for where in (me.x_up, me.x_down)]
        self.to_core(0, 1 - me.zl)

    def finish_half(self, half):
        for copy in self.far:
            copy.wait_recv()
        self.to_core(2, half)

    def wait_cores(self):
        for copy in self.cores:
            copy.wait_recv()


def gather_kernel(tok, gout, up, down, gain, T, G, U, D, N, local, send, recv):
    me = Place()
    peers = [lax.rem(me.f + k, 8) for k in range(1, 8)]
    meet(me.partners() + [{"fsdp": p} for p in peers])
    wires = Wires(send, recv)
    up_own = up.at[:, pl.ds(pl.multiple_of(me.zl * B, B), B)]
    down_own = down.at[pl.ds(pl.multiple_of(me.zl * B, B), B), :]
    u, d = WeightGather(me, wires, up_own, U), WeightGather(me, wires, down_own, D)
    t, g = TokenGather(me, wires, tok, T), TokenGather(me, wires, gout, G)
    u.start_z()
    u.start_y()
    t.start_own()
    gains = [wires.start(gain, N.at[me.f], {"fsdp": p}) for p in peers]
    own = me.rows = t.rows(me.zl)
    here = [
        pltpu.make_async_copy(src, dst, local.at[i])
        for i, (src, dst) in enumerate(
            [
                (up_own, U.at[me.s]),
                (down_own, D.at[me.s]),
                (tok, T.at[me.f, own]),
                (gout, G.at[me.f, own]),
                (gain, N.at[me.f]),
            ]
        )
    ]
    for copy in here:
        copy.start()
    d.start_z()
    t.forward(me.zl)
    t.start_other()
    g.start_own()
    u.forward_own()
    u.start_other()
    d.start_y()
    t.finish_half(me.zl)
    t.forward(1 - me.zl)
    g.forward(me.zl)
    g.start_other()
    t.finish_half(1 - me.zl)
    u.wait_far()
    u.forward_other()
    d.forward_own()
    d.start_other()
    g.finish_half(me.zl)
    g.forward(1 - me.zl)
    g.finish_half(1 - me.zl)
    u.wait_far_other()
    d.wait_far()
    d.forward_other()
    d.wait_far_other()
    t.wait_cores()
    g.wait_cores()
    for copy in gains:
        copy.wait_recv()
    for copy in here:
        copy.wait()
    wires.finish()


def gather(tok, gout, up, down, gain):
    blocks = jax.ShapeDtypeStruct((8, B, B), jnp.bfloat16)
    return pl.pallas_call(
        gather_kernel,
        out_shape=[blocks, blocks, blocks, blocks, jax.ShapeDtypeStruct((8, 8, B), jnp.float32)],
        in_specs=[pl.BlockSpec(memory_space=pl.ANY)] * 5,
        out_specs=[pl.BlockSpec(memory_space=pl.ANY)] * 5,
        scratch_shapes=[
            pltpu.SemaphoreType.DMA((5,)),
            pltpu.SemaphoreType.DMA((72,)),
            pltpu.SemaphoreType.DMA((72,)),
        ],
        compiler_params=pltpu.CompilerParams(collective_id=0, has_side_effects=True, vmem_limit_bytes=8 << 20),
        name="gather",
    )(tok, gout, up, down, gain)


def add(*parts):
    total = parts[0].astype(jnp.float32)
    for part in parts[1:]:
        total = total + part.astype(jnp.float32)
    return total


class RowScatter:
    def __init__(self, me, wires, terms, from_core, held, from_far, from_near, to_z, from_z):
        self.me, self.wires, self.terms = me, wires, terms
        self.from_core, self.held, self.from_far, self.from_near = from_core, held, from_far, from_near
        self.to_z, self.from_z = to_z, from_z

    def start_core(self):
        me = self.me
        self.core = {}
        for k in (2, 1, 3, 0):
            self.core[k] = self.wires.start(
                self.terms.at[me.feat(k, 1)], self.from_core.at[me.xs[k]], me.other_core
            )

    def join(self, k):
        self.core[k].wait_recv()
        me = self.me
        self.held[k] = add(self.terms[me.feat(k)], self.from_core[me.xs[k]]).astype(jnp.bfloat16)

    def start_far(self):
        me = self.me
        self.join(2)
        self.far = [
            self.wires.start(self.held.at[2, pl.ds(0, 256)], self.from_far.at[0], me.x_up),
            self.wires.start(self.held.at[2, pl.ds(256, 256)], self.from_far.at[1], me.x_down),
        ]
        self.join(1)
        self.join(3)
        self.join(0)

    def start_near(self):
        me, held = self.me, self.held
        self.far[0].wait_recv()
        held[1, :256] = add(held[1, :256], self.from_far[0]).astype(jnp.bfloat16)
        first = self.wires.start(held.at[1], self.from_near.at[0], me.x_up)
        self.far[1].wait_recv()
        held[3, 256:] = add(held[3, 256:], self.from_far[1]).astype(jnp.bfloat16)
        self.near = first, self.wires.start(held.at[3], self.from_near.at[1], me.x_down)

    def start_z(self):
        me = self.me
        self.near[0].wait_recv()
        self.near[1].wait_recv()
        rows = pl.ds(pl.multiple_of((1 - me.zl) * 256, 256), 256)
        self.to_z[...] = add(self.held[0, rows], self.from_near[0, rows], self.from_near[1, rows]).astype(jnp.bfloat16)
        self.z = self.wires.start(self.to_z, self.from_z, me.other_zl)

    def result(self):
        rows = pl.ds(pl.multiple_of(self.me.zl * 256, 256), 256)
        self.z.wait_recv()
        return add(self.held[0, rows], self.from_near[0, rows], self.from_near[1, rows], self.from_z[...])

    @staticmethod
    def scratch():
        blocks = lambda *shape: pltpu.VMEM(shape, jnp.bfloat16)
        return [blocks(4, B, B), blocks(4, B, B), blocks(2, 256, B), blocks(2, B, B), blocks(256, B), blocks(256, B)]


class WeightScatter:
    def __init__(self, me, wires, terms, held, from_far, from_near, to_z, from_z):
        self.me, self.wires, self.terms, self.held = me, wires, terms, held
        self.from_far, self.from_near, self.to_z, self.from_z = from_far, from_near, to_z, from_z

    def start_far(self):
        me, y = self.me, self.me.ys
        start = self.wires.start
        self.far = [
            start(self.terms.at[y[2]], self.from_far.at[0], me.y_up),
            start(self.terms.at[4 + y[2]], self.from_far.at[1], me.y_down),
        ]
        self.near = [
            start(self.terms.at[4 + y[1]], self.from_near.at[1], me.y_up),
            start(self.terms.at[y[3]], self.from_near.at[2], me.y_down),
        ]

    def start_near(self):
        me, y = self.me, self.me.ys
        start = self.wires.start
        self.far[0].wait_recv()
        self.held[0] = add(self.terms[y[1]], self.from_far[0]).astype(jnp.bfloat16)
        self.near.append(start(self.held.at[0], self.from_near.at[0], me.y_up))
        self.far[1].wait_recv()
        self.held[1] = add(self.terms[4 + y[3]], self.from_far[1]).astype(jnp.bfloat16)
        self.near.append(start(self.held.at[1], self.from_near.at[3], me.y_down))

    def total(self, zh):
        return add(self.terms[zh * 4 + self.me.y], self.from_near[zh], self.from_near[2 + zh])

    def start_z(self):
        for copy in self.near:
            copy.wait_recv()
        self.to_z[...] = self.total(1 - self.me.zh).astype(jnp.bfloat16)
        self.z = self.wires.start(self.to_z, self.from_z, self.me.other_zh)

    def start_out(self, out):
        self.z.wait_recv()
        out[...] = (self.total(self.me.zh) + self.from_z[...].astype(jnp.float32)).astype(jnp.bfloat16)
        self.last = self.wires.start(out, out, self.me.other_zl)

    def wait_out(self):
        self.last.wait_recv()

    @staticmethod
    def scratch():
        blocks = lambda *shape: pltpu.VMEM(shape, jnp.bfloat16)
        return [blocks(2, B, B), blocks(2, B, B), blocks(4, B, B), blocks(B, B), blocks(B, B)]


def scatter_kernel(branch, norm, g_up, g_down, branch_out, norm_out, up_out, down_out, *scratch):
    me = Place()
    meet(me.partners())
    send, recv = scratch[-2:]
    wires = Wires(send, recv)
    b = RowScatter(me, wires, branch, *scratch[0:6])
    n = RowScatter(me, wires, norm, *scratch[6:12])
    dn = WeightScatter(me, wires, g_down, *scratch[12:17])
    u = WeightScatter(me, wires, g_up, *scratch[17:22])
    dn.start_far()
    b.start_core()
    b.start_far()
    b.start_near()
    n.start_core()
    dn.start_near()
    u.start_far()
    n.start_far()
    n.start_near()
    b.start_z()
    dn.start_z()
    u.start_near()
    branch_out[...] = b.result()
    n.start_z()
    dn.start_out(down_out.at[me.zl])
    norm_out[...] = n.result()
    u.start_z()
    u.start_out(up_out.at[me.zl])
    dn.wait_out()
    u.wait_out()
    wires.finish()


def scatter(branch, norm, g_up, g_down):
    f32 = jax.ShapeDtypeStruct((256, B), jnp.float32)
    pair = jax.ShapeDtypeStruct((2, B, B), jnp.bfloat16)
    return pl.pallas_call(
        scatter_kernel,
        out_shape=[f32, f32, pair, pair],
        in_specs=[pl.BlockSpec(memory_space=pltpu.VMEM)] * 4,
        out_specs=[pl.BlockSpec(memory_space=pltpu.VMEM)] * 4,
        scratch_shapes=RowScatter.scratch() * 2
        + WeightScatter.scratch() * 2
        + [pltpu.SemaphoreType.DMA((40,)), pltpu.SemaphoreType.DMA((40,))],
        compiler_params=pltpu.CompilerParams(collective_id=1, has_side_effects=True, vmem_limit_bytes=60 << 20),
        name="scatter",
    )(branch, norm, g_up, g_down)


def with_halo(block):
    count = lax.axis_size("seq")
    forward = [(i, i + 1) for i in range(count - 1)]
    backward = [(target, source) for source, target in forward]
    low = lax.ppermute(block[:, 3:4], "seq", forward)
    high = lax.ppermute(block[:, 0:1], "seq", backward)
    return jnp.concatenate([low, block, high], axis=1)


def gelu_pair(preact):
    inner = gelu_scale * (preact + gelu_cubic * preact * preact * preact)
    tangent = jnp.tanh(inner)
    value = 0.5 * preact * (1.0 + tangent)
    slope = 0.5 * (1.0 + tangent) + 0.5 * preact * (1.0 - tangent * tangent) * gelu_scale * (
        1.0 + 3.0 * gelu_cubic * preact * preact
    )
    return (value, slope)


def pad_sides(field):
    return jnp.pad(field, ((0, 0), (0, 0), (1, 1), (1, 1), (0, 0)))


def conv_apply(padded, kernel, flipped):
    total = jnp.zeros((2, 4, 8, 8, padded.shape[4]), jnp.float32)
    for index in range(27):
        a, b, c = index // 9, index // 3 % 3, index % 3
        tap_row = kernel[26 - index] if flipped else kernel[index]
        window = padded[:, a : a + 4, b : b + 8, c : c + 8, :]
        total = total + tap_row * window.astype(jnp.float32)
    return total


def conv_grad(d_grid, padded):
    d_float = d_grid.astype(jnp.float32)
    collected = []
    for index in range(27):
        a, b, c = index // 9, index // 3 % 3, index % 3
        window = padded[:, a : a + 4, b : b + 8, c : c + 8, :]
        collected.append(jnp.sum(d_float * window.astype(jnp.float32), axis=(0, 1, 2, 3)))
    return jnp.stack(collected)


def per_device(tokens, grad_out, gain, up_weight, down_weight, conv_taps):
    zl, f = lax.axis_index("dp"), lax.axis_index("fsdp")
    tok = tokens.reshape(256, B)
    gout = grad_out.reshape(256, B)
    gain_rows = jnp.broadcast_to(gain[None], (8, B))
    T, G, U, D, N = gather(tok, gout, up_weight, down_weight, gain_rows)
    gain_all = N[:, 0:1, :]
    taps = lax.dynamic_slice_in_dim(conv_taps, zl * B, B, 1)
    flat = T.astype(jnp.float32)
    inverse = lax.rsqrt(jnp.sum(flat * flat, axis=(0, 2)) / 4096.0 + epsilon)[:, None]
    normed = (flat * inverse[None] * gain_all).astype(jnp.bfloat16)
    f32 = dict(preferred_element_type=jnp.float32)
    lifted = jnp.einsum("brd,bdh->rh", normed, U, **f32).astype(jnp.bfloat16)
    padded = pad_sides(with_halo(lifted.reshape(2, 4, 8, 8, B)))
    preact = conv_apply(padded, taps, False)
    value, slope = gelu_pair(preact)
    active = value.astype(jnp.bfloat16).reshape(512, B)
    branch_term = jnp.einsum("rh,bhd->brd", active, D, **f32).astype(jnp.bfloat16)
    d_active = jnp.einsum("brd,bhd->rh", G, D, **f32)
    down_term = jnp.einsum("rh,brd->bhd", active, G, **f32).astype(jnp.bfloat16)
    d_preact = (d_active * slope.reshape(512, B)).astype(jnp.bfloat16)
    d_grid = d_preact.reshape(2, 4, 8, 8, B)
    d_padded = pad_sides(with_halo(d_grid))
    d_lifted = conv_apply(d_padded, taps, True).astype(jnp.bfloat16).reshape(512, B)
    conv_term = conv_grad(d_grid, padded)
    up_term = jnp.einsum("brd,rh->bdh", normed, d_lifted, **f32).astype(jnp.bfloat16)
    norm_term = jnp.einsum("rh,bdh->brd", d_lifted, U, **f32).astype(jnp.bfloat16)
    branch, d_norm, g_up, g_down = scatter(branch_term, norm_term, up_term, down_term)
    own = tok.astype(jnp.float32)
    mixed = (own + branch).astype(jnp.bfloat16).reshape(tokens.shape)
    inv_own = lax.dynamic_slice_in_dim(inverse, zl * 256, 256, 0)
    hat = own * inv_own
    d_hat = d_norm * gain
    row_total = lax.psum(jnp.sum(d_hat * hat, axis=1), "fsdp")[:, None]
    grad_tokens = (
        (gout.astype(jnp.float32) + inv_own * (d_hat - hat * row_total / 4096.0))
        .astype(jnp.bfloat16)
        .reshape(tokens.shape)
    )
    wide = lax.dynamic_update_slice_in_dim(jnp.zeros((27, 1024), jnp.float32), conv_term, zl * B, 1)
    grad_conv, grad_gain = lax.psum((wide, jnp.sum(d_norm * hat, axis=0)), ("dp", "seq"))
    grad_up = g_up.transpose(1, 0, 2).reshape(512, 1024)
    grad_down = g_down.reshape(1024, 512)
    return (mixed, grad_tokens, grad_up, grad_down, grad_conv, grad_gain)


def solution(mesh):
    rows = P("dp", "seq", None, None, "fsdp")
    return jax.shard_map(
        per_device,
        mesh=mesh,
        in_specs=(rows, rows, P("fsdp"), P("seq", "fsdp"), P("fsdp", "seq"), P(None, "fsdp")),
        out_specs=(rows, rows, P("seq", "fsdp"), P("fsdp", "seq"), P(None, "fsdp"), P("fsdp")),
        check_vma=False,
    )
```

```python
import jax
import jax.numpy as jnp
from jax import lax
from jax.experimental import pallas as pl
from jax.experimental.pallas import tpu as pltpu
from jax.sharding import PartitionSpec as P

MESH = pl.DeviceIdType.MESH
gelu_scale = 0.7978845608028654
gelu_cubic = 0.044715
epsilon = 1e-06
B = 512


class Place:
    def __init__(self):
        self.zl = lax.axis_index("dp")
        self.f = lax.axis_index("fsdp")
        self.s = lax.axis_index("seq")
        self.x, self.c = lax.div(self.f, 2), lax.rem(self.f, 2)
        self.zh, self.y = lax.div(self.s, 4), lax.rem(self.s, 4)
        self.xs = [lax.rem(self.x + k, 4) for k in range(4)]
        self.ys = [lax.rem(self.y + k, 4) for k in range(4)]
        self.other_zl = {"dp": 1 - self.zl}
        self.other_core = {"fsdp": self.feat(0, 1)}
        self.x_up, self.x_down = {"fsdp": self.feat(1)}, {"fsdp": self.feat(3)}
        self.other_zh = {"seq": self.slab(0, 1)}
        self.y_up, self.y_down = {"seq": self.slab(1)}, {"seq": self.slab(3)}

    def feat(self, k, flip=0):
        return self.xs[k] * 2 + (1 - self.c if flip else self.c)

    def slab(self, k, flip=0):
        return (1 - self.zh if flip else self.zh) * 4 + self.ys[k]

    def partners(self):
        return [self.other_zl, self.other_core, self.x_up, self.x_down, self.other_zh, self.y_up, self.y_down]


class Wires:
    def __init__(self, send, recv):
        self.send, self.recv, self.copies, self.left = send, recv, [], 0

    def start(self, src, dst, where):
        i = len(self.copies)
        copy = pltpu.make_async_remote_copy(
            src_ref=src, dst_ref=dst, send_sem=self.send.at[i], recv_sem=self.recv.at[i],
            device_id=where, device_id_type=MESH,
        )
        copy.start()
        self.copies.append(copy)
        return copy

    def flush(self, until=None):
        for copy in self.copies[self.left : until]:
            copy.wait_send()
        self.left = len(self.copies) if until is None else until


def meet(partners):
    barrier = pltpu.get_barrier_semaphore()
    for where in partners:
        pl.semaphore_signal(barrier, inc=1, device_id=where, device_id_type=MESH)
    pl.semaphore_wait(barrier, len(partners))


class WeightGather:
    def __init__(self, me, wires, own, buf):
        self.me, self.wires, self.own, self.buf = me, wires, own, buf

    def start_z(self):
        self.z = self.wires.start(self.own, self.buf.at[self.me.s], self.me.other_zh)

    def start_y(self):
        self.up = self.wires.start(self.own, self.buf.at[self.me.s], self.me.y_up)
        self.down = self.wires.start(self.own, self.buf.at[self.me.s], self.me.y_down)

    def forward(self, flip):
        me, buf = self.me, self.buf
        below, above = me.slab(3, flip), me.slab(1, flip)
        self.up.wait_recv()
        part = buf.at[below, pl.ds(0, B // 2)]
        first = self.wires.start(part, part, me.y_up)
        self.down.wait_recv()
        part = buf.at[above, pl.ds(B // 2, B // 2)]
        return first, self.wires.start(part, part, me.y_down)

    def forward_own(self):
        self.far = self.forward(0)

    def start_other(self):
        self.z.wait_recv()
        block = self.buf.at[self.me.slab(0, 1)]
        self.up = self.wires.start(block, block, self.me.y_up)
        self.down = self.wires.start(block, block, self.me.y_down)

    def forward_other(self):
        self.far_other = self.forward(1)

    def wait_far(self):
        for copy in self.far:
            copy.wait_recv()

    def wait_far_other(self):
        for copy in self.far_other:
            copy.wait_recv()


class TokenGather:
    def __init__(self, me, wires, own, buf):
        self.me, self.wires, self.own, self.buf = me, wires, own, buf
        self.cores = []

    def rows(self, half, part=None):
        if part is None:
            return pl.ds(pl.multiple_of(half * 256, 256), 256)
        return pl.ds(pl.multiple_of(half * 256 + part * 128, 128), 128)

    def start_own(self):
        me = self.me
        dst = self.buf.at[me.f, self.rows(me.zl)]
        self.z = self.wires.start(self.own, dst, me.other_zl)
        self.ring = [self.wires.start(self.own, dst, where) for where in (me.x_up, me.x_down)]
        self.cores.append(self.wires.start(self.own, dst, me.other_core))

    def to_core(self, k, half):
        block = self.buf.at[self.me.feat(k), self.rows(half)]
        self.cores.append(self.wires.start(block, block, self.me.other_core))

    def forward(self, half):
        me, buf, ring = self.me, self.buf, self.ring
        ring[0].wait_recv()
        part = buf.at[me.feat(3), self.rows(half, 0)]
        first = self.wires.start(part, part, me.x_up)
        ring[1].wait_recv()
        part = buf.at[me.feat(1), self.rows(half, 1)]
        self.far = first, self.wires.start(part, part, me.x_down)
        self.to_core(3, half)
        self.to_core(1, half)

    def start_other(self):
        me = self.me
        self.z.wait_recv()
        block = self.buf.at[me.f, self.rows(1 - me.zl)]
        self.ring = [self.wires.start(block, block, where) for where in (me.x_up, me.x_down)]
        self.to_core(0, 1 - me.zl)

    def finish_half(self, half):
        for copy in self.far:
            copy.wait_recv()
        self.to_core(2, half)

    def wait_cores(self):
        for copy in self.cores:
            copy.wait_recv()


CHUNK = 64


def chunk(r, base=0):
    return pl.ds(pl.multiple_of(base + r * CHUNK, CHUNK), CHUNK)


def loop(count, body):
    def step(i, carry):
        body(i)
        return carry

    lax.fori_loop(0, count, step, 0)


def add_into(dst, *parts):
    def body(r):
        rows = chunk(r)
        total = parts[0][rows, :].astype(jnp.float32)
        for part in parts[1:]:
            total = total + part[rows, :].astype(jnp.float32)
        dst[rows, :] = total.astype(dst.dtype)

    loop(dst.shape[0] // CHUNK, body)


class RowScatter:
    def __init__(self, me, wires, terms, from_core, from_far, from_near, to_z, from_z):
        self.me, self.wires, self.terms = me, wires, terms
        self.from_core, self.from_far, self.from_near = from_core, from_far, from_near
        self.to_z, self.from_z = to_z, from_z

    def start_core(self):
        me = self.me
        self.core = {}
        for k in (2, 1, 3, 0):
            self.core[k] = self.wires.start(
                self.terms.at[me.feat(k, 1)], self.from_core.at[me.xs[k]], me.other_core
            )

    def held(self, k):
        return self.terms.at[self.me.feat(k)]

    def join(self, k):
        self.core[k].wait_recv()
        add_into(self.held(k), self.held(k), self.from_core.at[self.me.xs[k]])

    def start_far(self):
        me = self.me
        self.join(2)
        self.far = [
            self.wires.start(self.held(2).at[pl.ds(0, 256)], self.from_far.at[0], me.x_up),
            self.wires.start(self.held(2).at[pl.ds(256, 256)], self.from_far.at[1], me.x_down),
        ]
        self.join(1)
        self.join(3)
        self.join(0)

    def start_near(self):
        me = self.me
        self.far[0].wait_recv()
        part = self.held(1).at[pl.ds(0, 256)]
        add_into(part, part, self.from_far.at[0])
        first = self.wires.start(self.held(1), self.from_near.at[0], me.x_up)
        self.far[1].wait_recv()
        part = self.held(3).at[pl.ds(256, 256)]
        add_into(part, part, self.from_far.at[1])
        self.near = first, self.wires.start(self.held(3), self.from_near.at[1], me.x_down)

    def half(self, zl):
        rows = pl.ds(pl.multiple_of(zl * 256, 256), 256)
        return [self.held(0).at[rows], self.from_near.at[0, rows], self.from_near.at[1, rows]]

    def start_z(self):
        me = self.me
        self.near[0].wait_recv()
        self.near[1].wait_recv()
        add_into(self.to_z, *self.half(1 - me.zl))
        self.z = self.wires.start(self.to_z, self.from_z, me.other_zl)

    def wait(self):
        self.z.wait_recv()
        self.parts = self.half(self.me.zl) + [self.from_z]

    def result(self, rows):
        total = self.parts[0][rows, :].astype(jnp.float32)
        for part in self.parts[1:]:
            total = total + part[rows, :].astype(jnp.float32)
        return total

    @staticmethod
    def scratch():
        blocks = lambda *shape: pltpu.VMEM(shape, jnp.bfloat16)
        return [blocks(4, B, B), blocks(2, 256, B), blocks(2, B, B), blocks(256, B), blocks(256, B)]


class WeightScatter:
    def __init__(self, me, wires, terms, from_far, from_near, to_z, from_z):
        self.me, self.wires, self.terms = me, wires, terms
        self.from_far, self.from_near, self.to_z, self.from_z = from_far, from_near, to_z, from_z

    def start_far(self):
        me, y = self.me, self.me.ys
        start = self.wires.start
        self.far = [
            start(self.terms.at[y[2]], self.from_far.at[0], me.y_up),
            start(self.terms.at[4 + y[2]], self.from_far.at[1], me.y_down),
        ]
        self.near = [
            start(self.terms.at[4 + y[1]], self.from_near.at[1], me.y_up),
            start(self.terms.at[y[3]], self.from_near.at[2], me.y_down),
        ]

    def start_near(self):
        me, y = self.me, self.me.ys
        start = self.wires.start
        self.far[0].wait_recv()
        block = self.terms.at[y[1]]
        add_into(block, block, self.from_far.at[0])
        self.near.append(start(block, self.from_near.at[0], me.y_up))
        self.far[1].wait_recv()
        block = self.terms.at[4 + y[3]]
        add_into(block, block, self.from_far.at[1])
        self.near.append(start(block, self.from_near.at[3], me.y_down))

    def parts(self, zh):
        return [self.terms.at[zh * 4 + self.me.y], self.from_near.at[zh], self.from_near.at[2 + zh]]

    def start_z(self):
        for copy in self.near:
            copy.wait_recv()
        add_into(self.to_z, *self.parts(1 - self.me.zh))
        self.z = self.wires.start(self.to_z, self.from_z, self.me.other_zh)

    def start_out(self, out, sem):
        self.z.wait_recv()
        block = self.terms.at[self.me.s]
        add_into(block, *self.parts(self.me.zh), self.from_z)
        self.last = self.wires.start(block, out, self.me.other_zl)
        self.here = pltpu.make_async_copy(block, out, sem)
        self.here.start()

    def wait_out(self):
        self.last.wait_recv()
        self.here.wait()

    @staticmethod
    def scratch():
        blocks = lambda *shape: pltpu.VMEM(shape, jnp.bfloat16)
        return [blocks(2, B, B), blocks(4, B, B), blocks(B, B), blocks(B, B)]


class Halo:
    def __init__(self, me, wires, planes, came, field):
        self.me, self.wires, self.planes, self.came, self.field = me, wires, planes, came, field

    def start(self):
        me = self.me
        above, below = {"seq": lax.rem(me.s + 1, 8)}, {"seq": lax.rem(me.s + 7, 8)}
        self.copies = [
            self.wires.start(self.planes.at[1], self.came.at[0], above),
            self.wires.start(self.planes.at[0], self.came.at[1], below),
        ]

    def wait(self):
        edges = [(me_s != edge).astype(jnp.float32) for me_s, edge in ((self.me.s, 0), (self.me.s, 7))]
        for copy in self.copies:
            copy.wait_recv()
        for side in range(2):
            for snap in range(2):
                plane = self.came[side, snap].astype(jnp.float32) * edges[side]
                self.field[snap * 6 + side * 5, 1:9] = plane.reshape(8, 8, B)


def spread(total, field, planes):
    def body(i):
        snap, p = lax.div(i, 4), lax.rem(i, 4)
        rounded = total[chunk(i), :].astype(jnp.bfloat16)
        field[snap * 6 + 1 + p, 1:9] = rounded.astype(jnp.float32).reshape(8, 8, B)

    loop(8, body)
    for side in range(2):
        for snap in range(2):
            planes[side, snap] = total[pl.ds(snap * 256 + side * 192, 64), :].astype(jnp.bfloat16)


def shift(value, by):
    cells = lax.broadcasted_iota(jnp.int32, value.shape, 1)
    moved = pltpu.roll(value, by % 8, 1)
    return jnp.where(cells == (0 if by == 1 else 7), 0.0, moved)


def conv_planes(field, taps, flipped, count, which, finish):
    def body(i):
        snap, p = which(i)
        for lane in range(0, B, 128):
            lanes = pl.ds(lane, 128)
            by_c = [None] * 3
            for a in range(3):
                for b in range(3):
                    window = field[snap * 6 + p + a, pl.ds(b, 8), :, lanes]
                    for c in range(3):
                        index = a * 9 + b * 3 + c
                        index = 26 - index if flipped else index
                        term = window * taps[pl.ds(index, 1), lanes].reshape(1, 1, 128)
                        by_c[c] = term if by_c[c] is None else by_c[c] + term
            total = by_c[1] + shift(by_c[0], 1) + shift(by_c[2], -1)
            finish(chunk(snap * 4 + p), lanes, total.reshape(CHUNK, 128))

    loop(count, body)


def inner(i):
    return lax.div(i, 2), 1 + lax.rem(i, 2)


def outer(i):
    return lax.div(i, 2), 3 * lax.rem(i, 2)


def gelu_pair(preact):
    inner_value = gelu_scale * (preact + gelu_cubic * preact * preact * preact)
    tangent = jnp.tanh(inner_value)
    value = 0.5 * preact * (1.0 + tangent)
    slope = 0.5 * (1.0 + tangent) + 0.5 * preact * (1.0 - tangent * tangent) * gelu_scale * (
        1.0 + 3.0 * gelu_cubic * preact * preact
    )
    return (value, slope)


def dot(left, right, left_dim, right_dim):
    return lax.dot_general(
        left, right, (((left_dim,), (right_dim,)), ((), ())), preferred_element_type=jnp.float32
    )


def block_kernel(
    tok, gout, gain, up, down, taps_all,
    mixed_out, tokens_out, up_out, down_out, conv_out, gain_out,
    T, G, U, D, N, PB, GD, gains, taps, field, d_field, total, slope, active, d_lifted, inverse,
    planes, came, d_norm, row_part, conv_sums, conv_terms, row_terms, gain_terms,
    b0, b1, b2, b3, b4, n0, n1, n2, n3, n4, w0, w1, w2, w3, v0, v1, v2, v3,
    local, send, recv,
):
    me = Place()
    group = me.zl * 8 + me.s
    peers = [lax.rem(me.f + k, 8) for k in range(1, 8)]
    slabs = [lax.rem(me.s + k, 8) for k in range(1, 8)]
    groups = [lax.rem(group + k, 16) for k in range(1, 16)]
    groups = [(k, {"dp": lax.div(k, 8), "seq": lax.rem(k, 8)}) for k in groups]
    meet([{"fsdp": p} for p in peers] + [where for _, where in groups])
    wires = Wires(send, recv)
    hidden = pl.ds(pl.multiple_of(me.zl * B, B), B)
    up_own, down_own = up.at[:, hidden], down.at[hidden, :]
    u, d = WeightGather(me, wires, up_own, U), WeightGather(me, wires, down_own, D)
    t, g = TokenGather(me, wires, tok, T), TokenGather(me, wires, gout, G)
    PN, GU = T, D
    b = RowScatter(me, wires, PB, b0, b1, b2, b3, b4)
    n = RowScatter(me, wires, PN, n0, n1, n2, n3, n4)
    gd = WeightScatter(me, wires, GD, w0, w1, w2, w3)
    gu = WeightScatter(me, wires, GU, v0, v1, v2, v3)

    u.start_z()
    u.start_y()
    t.start_own()
    gain_copies = [wires.start(gain, gains.at[me.f], {"fsdp": p}) for p in peers]
    own = t.rows(me.zl)
    here = [
        pltpu.make_async_copy(src, dst, local.at[i])
        for i, (src, dst) in enumerate(
            [
                (tok, T.at[me.f, own]),
                (gain, gains.at[me.f]),
                (up_own, U.at[me.s]),
                (taps_all.at[:, hidden], taps),
                (gout, G.at[me.f, own]),
                (down_own, D.at[me.s]),
            ]
        )
    ]
    for copy in here:
        copy.start()
    field[...] = jnp.zeros_like(field)
    d_field[...] = jnp.zeros_like(d_field)
    t.forward(me.zl)
    t.start_other()
    d.start_z()
    g.start_own()
    u.forward_own()
    u.start_other()
    d.start_y()
    t.finish_half(me.zl)
    t.forward(1 - me.zl)
    t.finish_half(1 - me.zl)
    for copy in here:
        copy.wait()
    for copy in gain_copies:
        copy.wait_recv()
    g.forward(me.zl)
    g.start_other()
    t.wait_cores()

    def normalise(r):
        rows = chunk(r)
        squares = jnp.zeros((CHUNK, 128), jnp.float32)
        for k in range(8):
            for lane in range(0, B, 128):
                value = T[k, rows, pl.ds(lane, 128)].astype(jnp.float32)
                squares = squares + value * value
        mean = jnp.sum(squares, axis=1, keepdims=True) / 4096.0
        inv = jnp.broadcast_to(lax.rsqrt(mean + epsilon), (CHUNK, 128))
        inverse[rows, :] = inv
        for k in range(8):
            for lane in range(0, B, 128):
                lanes = pl.ds(lane, 128)
                value = T[k, rows, lanes].astype(jnp.float32) * inv * gains[k, 0:1, lanes]
                N[k, rows, lanes] = value.astype(jnp.bfloat16)

    loop(8, normalise)
    total[...] = jnp.zeros_like(total)

    def lift(zh):
        def body(i):
            j = zh * 4 + i
            total[...] += dot(N[j], U[j], 1, 0)

        loop(4, body)

    u.wait_far()
    u.forward_other()
    lift(me.zh)
    d.forward_own()
    d.start_other()
    g.finish_half(me.zl)
    g.forward(1 - me.zl)
    u.wait_far_other()
    lift(1 - me.zh)
    spread(total, field, planes.at[0])
    halo = Halo(me, wires, planes.at[0], came.at[0], field)
    halo.start()

    def activate(rows, lanes, preact):
        value, rate = gelu_pair(preact)
        active[rows, lanes] = value.astype(jnp.bfloat16)
        slope[rows, lanes] = rate

    conv_planes(field, taps, False, 4, inner, activate)
    g.finish_half(1 - me.zl)
    halo.wait()
    conv_planes(field, taps, False, 4, outer, activate)
    g.wait_cores()

    def down_term(j):
        GD[j] = dot(active[...], G[j], 0, 0).astype(jnp.bfloat16)

    loop(8, down_term)
    d.wait_far()
    d.forward_other()
    gathered = len(wires.copies)
    gd.start_far()
    total[...] = jnp.zeros_like(total)

    def d_active(zh):
        def body(i):
            j = zh * 4 + i
            total[...] += dot(G[j], D[j], 1, 1)

        loop(4, body)

    d_active(me.zh)
    d.wait_far_other()
    d_active(1 - me.zh)

    def d_preact(r):
        total[chunk(r), :] = total[chunk(r), :] * slope[chunk(r), :]

    loop(8, d_preact)
    spread(total, d_field, planes.at[1])
    d_halo = Halo(me, wires, planes.at[1], came.at[1], d_field)
    d_halo.start()

    def branch_term(j):
        PB[j] = dot(active[...], D[j], 1, 0).astype(jnp.bfloat16)

    loop(8, branch_term)
    b.start_core()

    def d_lift(rows, lanes, value):
        d_lifted[rows, lanes] = value.astype(jnp.bfloat16)

    conv_planes(d_field, taps, True, 4, inner, d_lift)
    d_halo.wait()
    conv_planes(d_field, taps, True, 4, outer, d_lift)
    b.start_far()
    gd.start_near()
    wires.flush(gathered)

    def up_term(j):
        GU[j] = dot(N[j], d_lifted[...], 0, 0).astype(jnp.bfloat16)

    loop(8, up_term)
    gu.start_far()

    def norm_term(j):
        PN[j] = dot(d_lifted[...], U[j], 1, 1).astype(jnp.bfloat16)

    loop(8, norm_term)
    n.start_core()
    b.start_near()
    n.start_far()
    gd.start_z()

    conv_sums[...] = jnp.zeros_like(conv_sums)

    def taps_grad(i):
        snap, p = lax.div(i, 4), lax.rem(i, 4)
        for lane in range(0, B, 128):
            lanes = pl.ds(lane, 128)
            here_d = d_field[snap * 6 + 1 + p, pl.ds(1, 8), :, lanes]
            by_c = [shift(here_d, -1), here_d, shift(here_d, 1)]
            for a in range(3):
                for b_ in range(3):
                    window = field[snap * 6 + p + a, pl.ds(b_, 8), :, lanes]
                    for c in range(3):
                        term = jnp.sum(by_c[c] * window, axis=0)
                        conv_sums[a * 9 + b_ * 3 + c, :, lanes] += term

    loop(8, taps_grad)
    conv_terms[me.s] = jnp.sum(conv_sums[...], axis=1).astype(jnp.bfloat16)
    conv_copies = [wires.start(conv_terms.at[me.s], conv_terms.at[me.s], {"seq": k}) for k in slabs]

    b.start_z()
    n.start_near()
    gd.start_out(down_out.at[hidden, :], local.at[0])
    gu.start_near()
    b.wait()

    def mix(r):
        rows = chunk(r)
        mixed_out[rows, :] = (tok[rows, :].astype(jnp.float32) + b.result(rows)).astype(jnp.bfloat16)

    loop(4, mix)
    for copy in conv_copies:
        copy.wait_recv()
    conv = conv_terms[0].astype(jnp.float32)
    for k in range(1, 8):
        conv = conv + conv_terms[k].astype(jnp.float32)
    conv_out[me.zl] = conv
    conv_copy = wires.start(conv_out.at[me.zl], conv_out.at[me.zl], me.other_zl)
    n.start_z()
    n.wait()

    def rows_part(r, gain_sum):
        rows = chunk(r)
        whole = n.result(rows)
        d_norm[rows, :] = whole
        inv = inverse[chunk(r, me.zl * 256), :]
        part = jnp.zeros((CHUNK, 128), jnp.float32)
        sums = []
        for lane in range(0, B, 128):
            lanes = slice(lane, lane + 128)
            with_hat = whole[:, lanes] * (tok[rows, lanes].astype(jnp.float32) * inv)
            part = part + with_hat * gain[0:1, lanes]
            sums.append(jnp.sum(with_hat.reshape(8, 8, 128), axis=0))
        row_part[rows, :] = part
        return gain_sum + jnp.concatenate(sums, axis=1)

    gain_sum = lax.fori_loop(0, 4, rows_part, jnp.zeros((8, B), jnp.float32))
    row_sum = jnp.sum(jnp.transpose(row_part[...]), axis=0, keepdims=True)
    row_terms[me.f] = jnp.broadcast_to(row_sum, (8, 256))
    row_copies = [wires.start(row_terms.at[me.f], row_terms.at[me.f], {"fsdp": p}) for p in peers]
    gain_terms[group] = jnp.broadcast_to(jnp.sum(gain_sum, axis=0, keepdims=True), (8, B))
    last_copies = [wires.start(gain_terms.at[group], gain_terms.at[group], where) for _, where in groups]

    gu.start_z()
    for copy in row_copies:
        copy.wait_recv()
    rows_sum = row_terms[0]
    for k in range(1, 8):
        rows_sum = rows_sum + row_terms[k]
    row_part[...] = jnp.transpose(jnp.broadcast_to(rows_sum[0:1, :], (128, 256)))

    def finish(r):
        rows = chunk(r)
        inv = inverse[chunk(r, me.zl * 256), :]
        share = row_part[rows, :] / 4096.0
        for lane in range(0, B, 128):
            lanes = slice(lane, lane + 128)
            hat = tok[rows, lanes].astype(jnp.float32) * inv
            value = inv * (d_norm[rows, lanes] * gain[0:1, lanes] - hat * share)
            tokens_out[rows, lanes] = (gout[rows, lanes].astype(jnp.float32) + value).astype(jnp.bfloat16)

    loop(4, finish)
    gu.start_out(up_out.at[:, hidden], local.at[1])
    for copy in last_copies:
        copy.wait_recv()
    all_gain = gain_terms[0]
    for k in range(1, 16):
        all_gain = all_gain + gain_terms[k]
    gain_out[...] = all_gain
    conv_copy.wait_recv()
    gd.wait_out()
    gu.wait_out()
    wires.flush()


def block(tok, gout, gain, up, down, taps):
    vmem = pl.BlockSpec(memory_space=pltpu.VMEM)
    anywhere = pl.BlockSpec(memory_space=pl.ANY)
    bf16, f32 = jnp.bfloat16, jnp.float32
    blocks = pltpu.VMEM((8, B, B), bf16)
    padded = pltpu.VMEM((12, 10, 8, B), f32)
    return pl.pallas_call(
        block_kernel,
        out_shape=[
            jax.ShapeDtypeStruct((256, B), bf16),
            jax.ShapeDtypeStruct((256, B), bf16),
            jax.ShapeDtypeStruct((B, 2 * B), bf16),
            jax.ShapeDtypeStruct((2 * B, B), bf16),
            jax.ShapeDtypeStruct((2, 32, B), f32),
            jax.ShapeDtypeStruct((8, B), f32),
        ],
        in_specs=[vmem, vmem, vmem, anywhere, anywhere, anywhere],
        out_specs=[vmem, vmem, anywhere, anywhere, vmem, vmem],
        scratch_shapes=[blocks] * 7
        + [
            pltpu.VMEM((8, 8, B), f32),
            pltpu.VMEM((27, B), f32),
            padded,
            padded,
            pltpu.VMEM((B, B), f32),
            pltpu.VMEM((B, B), f32),
            pltpu.VMEM((B, B), bf16),
            pltpu.VMEM((B, B), bf16),
            pltpu.VMEM((B, 128), f32),
            pltpu.VMEM((2, 2, 2, CHUNK, B), bf16),
            pltpu.VMEM((2, 2, 2, CHUNK, B), bf16),
            pltpu.VMEM((256, B), f32),
            pltpu.VMEM((256, 128), f32),
            pltpu.VMEM((32, 8, B), f32),
            pltpu.VMEM((8, 32, B), bf16),
            pltpu.VMEM((8, 8, 256), f32),
            pltpu.VMEM((16, 8, B), f32),
        ]
        + RowScatter.scratch() * 2
        + WeightScatter.scratch() * 2
        + [pltpu.SemaphoreType.DMA((6,)), pltpu.SemaphoreType.DMA((144,)), pltpu.SemaphoreType.DMA((144,))],
        compiler_params=pltpu.CompilerParams(
            collective_id=0, has_side_effects=True, vmem_limit_bytes=62 << 20
        ),
        name="block",
    )(tok, gout, gain, up, down, taps)


def per_device(tokens, grad_out, gain, up_weight, down_weight, conv_taps):
    tok = tokens.reshape(256, B)
    gout = grad_out.reshape(256, B)
    gain_rows = jnp.broadcast_to(gain[None], (8, B))
    mixed, grad_tokens, grad_up, grad_down, conv, last = block(
        tok, gout, gain_rows, up_weight, down_weight, conv_taps
    )
    grad_conv = conv[:, :27].transpose(1, 0, 2).reshape(27, 2 * B)
    return (
        mixed.reshape(tokens.shape),
        grad_tokens.reshape(tokens.shape),
        grad_up,
        grad_down,
        grad_conv,
        last[0],
    )


def solution(mesh):
    rows = P("dp", "seq", None, None, "fsdp")
    return jax.shard_map(
        per_device,
        mesh=mesh,
        in_specs=(rows, rows, P("fsdp"), P("seq", "fsdp"), P("fsdp", "seq"), P(None, "fsdp")),
        out_specs=(rows, rows, P("seq", "fsdp"), P("fsdp", "seq"), P(None, "fsdp"), P("fsdp")),
        check_vma=False,
    )
```

```python
import jax
import jax.numpy as jnp
from jax import lax
from jax.experimental import pallas as pl
from jax.experimental.pallas import tpu as pltpu
from jax.sharding import PartitionSpec as P

MESH = pl.DeviceIdType.MESH
gelu_scale = 0.7978845608028654
gelu_cubic = 0.044715
epsilon = 1e-06
B = 512


class Place:
    def __init__(self):
        self.zl = lax.axis_index("dp")
        self.f = lax.axis_index("fsdp")
        self.s = lax.axis_index("seq")
        self.x, self.c = lax.div(self.f, 2), lax.rem(self.f, 2)
        self.zh, self.y = lax.div(self.s, 4), lax.rem(self.s, 4)
        self.xs = [lax.rem(self.x + k, 4) for k in range(4)]
        self.ys = [lax.rem(self.y + k, 4) for k in range(4)]
        self.other_zl = {"dp": 1 - self.zl}
        self.other_core = {"fsdp": self.feat(0, 1)}
        self.x_up, self.x_down = {"fsdp": self.feat(1)}, {"fsdp": self.feat(3)}
        self.other_zh = {"seq": self.slab(0, 1)}
        self.y_up, self.y_down = {"seq": self.slab(1)}, {"seq": self.slab(3)}
        self.x_far, self.y_far = {"fsdp": self.feat(2)}, {"seq": self.slab(2)}
        self.diagonal = {"dp": 1 - self.zl, "seq": self.slab(0, 1)}
        self.rb = self.zl * 2 + self.zh
        self.z_peers = [
            (self.other_zl, (1 - self.zl) * 2 + self.zh),
            (self.other_zh, self.zl * 2 + 1 - self.zh),
            (self.diagonal, 3 - self.rb),
        ]
        self.x_peers = [self.x_up, self.x_far, self.x_down]
        self.y_peers = [self.y_up, self.y_far, self.y_down]

    def feat(self, k, flip=0):
        return self.xs[k] * 2 + (1 - self.c if flip else self.c)

    def slab(self, k, flip=0):
        return (1 - self.zh if flip else self.zh) * 4 + self.ys[k]

    def partners(self):
        return self.x_peers + self.y_peers + [where for where, _ in self.z_peers] + [self.other_core]


class Wires:
    def __init__(self, send, recv):
        self.send, self.recv, self.copies, self.left = send, recv, [], 0

    def start(self, src, dst, where):
        i = len(self.copies)
        copy = pltpu.make_async_remote_copy(
            src_ref=src, dst_ref=dst, send_sem=self.send.at[i], recv_sem=self.recv.at[i],
            device_id=where, device_id_type=MESH,
        )
        copy.start()
        self.copies.append(copy)
        return copy

    def flush(self, until=None):
        for copy in self.copies[self.left : until]:
            copy.wait_send()
        self.left = len(self.copies) if until is None else until


def meet(partners):
    barrier = pltpu.get_barrier_semaphore()
    for where in partners:
        pl.semaphore_signal(barrier, inc=1, device_id=where, device_id_type=MESH)
    pl.semaphore_wait(barrier, len(partners))


class WeightGather:
    def __init__(self, me, wires, own, for_other, buf):
        self.me, self.wires, self.own, self.for_other, self.buf = me, wires, own, for_other, buf
        self.half = buf.shape[1] // 2

    def start_z(self):
        self.z = self.wires.start(self.for_other, self.buf.at[self.me.s], self.me.other_zh)

    def start_y(self):
        self.up = self.wires.start(self.own, self.buf.at[self.me.s], self.me.y_up)
        self.down = self.wires.start(self.own, self.buf.at[self.me.s], self.me.y_down)

    def forward(self, flip):
        me, buf = self.me, self.buf
        below, above = me.slab(3, flip), me.slab(1, flip)
        self.up.wait_recv()
        part = buf.at[below, pl.ds(0, self.half)]
        first = self.wires.start(part, part, me.y_up)
        self.down.wait_recv()
        part = buf.at[above, pl.ds(self.half, self.half)]
        return first, self.wires.start(part, part, me.y_down)

    def forward_own(self):
        self.far = self.forward(0)

    def start_other(self):
        self.z.wait_recv()
        block = self.buf.at[self.me.slab(0, 1)]
        self.up = self.wires.start(block, block, self.me.y_up)
        self.down = self.wires.start(block, block, self.me.y_down)

    def forward_other(self):
        self.far_other = self.forward(1)

    def wait_far(self):
        for copy in self.far:
            copy.wait_recv()

    def wait_far_other(self):
        for copy in self.far_other:
            copy.wait_recv()


class TokenGather:
    def __init__(self, me, wires, own, buf, part, partners):
        self.me, self.wires, self.own, self.buf = me, wires, own, buf
        self.partners = [where for where, _ in partners]
        self.parts = [part] + [place for _, place in partners]
        self.ring, self.far, self.cores = {}, {}, []

    def rows(self, i, half=None):
        if half is None:
            return pl.ds(pl.multiple_of(self.parts[i] * 256, 256), 256)
        return pl.ds(pl.multiple_of(self.parts[i] * 256 + half * 128, 128), 128)

    def start_z(self):
        dst = self.buf.at[self.me.f, self.rows(0)]
        self.z = [self.wires.start(self.own, dst, where) for where in self.partners]

    def start(self, i):
        me = self.me
        dst = self.buf.at[me.f, self.rows(i)]
        src = dst if i else self.own
        if i:
            self.z[i - 1].wait_recv()
        self.ring[i] = [self.wires.start(src, dst, where) for where in (me.x_up, me.x_down)]
        self.cores.append(self.wires.start(src, dst, me.other_core))

    def to_core(self, k, i):
        block = self.buf.at[self.me.feat(k), self.rows(i)]
        self.cores.append(self.wires.start(block, block, self.me.other_core))

    def forward(self, i):
        me, buf = self.me, self.buf
        self.ring[i][0].wait_recv()
        part = buf.at[me.feat(3), self.rows(i, 0)]
        first = self.wires.start(part, part, me.x_up)
        self.ring[i][1].wait_recv()
        part = buf.at[me.feat(1), self.rows(i, 1)]
        self.far[i] = first, self.wires.start(part, part, me.x_down)
        self.to_core(3, i)
        self.to_core(1, i)

    def finish(self, i):
        for copy in self.far[i]:
            copy.wait_recv()
        self.to_core(2, i)

    def wait_cores(self):
        for copy in self.cores:
            copy.wait_recv()


CHUNK = 64
HID = 256


def chunk(r, base=0):
    return pl.ds(pl.multiple_of(base + r * CHUNK, CHUNK), CHUNK)


def loop(count, body):
    def step(i, carry):
        body(i)
        return carry

    lax.fori_loop(0, count, step, 0)


def add_into(dst, *parts):
    def body(r):
        rows = chunk(r)
        total = parts[0][rows, :].astype(jnp.float32)
        for part in parts[1:]:
            total = total + part[rows, :].astype(jnp.float32)
        dst[rows, :] = total.astype(dst.dtype)

    loop(dst.shape[0] // CHUNK, body)


class RowScatter:
    def __init__(self, me, wires, terms, part, partners, from_core, from_far, from_near, from_z):
        self.me, self.wires, self.terms = me, wires, terms
        self.part, self.partners = part, partners
        self.from_core, self.from_far, self.from_near = from_core, from_far, from_near
        self.from_z = from_z
        self.side = terms.shape[1] // 2

    def start_core(self):
        me = self.me
        self.core = {}
        for k in (2, 1, 3, 0):
            self.core[k] = self.wires.start(
                self.terms.at[me.feat(k, 1)], self.from_core.at[me.xs[k]], me.other_core
            )

    def held(self, k):
        return self.terms.at[self.me.feat(k)]

    def join(self, k):
        self.core[k].wait_recv()
        add_into(self.held(k), self.held(k), self.from_core.at[self.me.xs[k]])

    def start_far(self):
        me, side = self.me, self.side
        self.join(2)
        self.far = [
            self.wires.start(self.held(2).at[pl.ds(0, side)], self.from_far.at[0], me.x_up),
            self.wires.start(self.held(2).at[pl.ds(side, side)], self.from_far.at[1], me.x_down),
        ]
        self.join(1)
        self.join(3)
        self.near = [
            self.wires.start(self.held(1).at[pl.ds(side, side)], self.from_near.at[0, pl.ds(side, side)], me.x_up),
            self.wires.start(self.held(3).at[pl.ds(0, side)], self.from_near.at[1, pl.ds(0, side)], me.x_down),
        ]
        self.join(0)

    def start_near(self):
        me, side = self.me, self.side
        self.far[0].wait_recv()
        part = self.held(1).at[pl.ds(0, side)]
        add_into(part, part, self.from_far.at[0])
        self.near.append(self.wires.start(part, self.from_near.at[0, pl.ds(0, side)], me.x_up))
        self.far[1].wait_recv()
        part = self.held(3).at[pl.ds(side, side)]
        add_into(part, part, self.from_far.at[1])
        self.near.append(self.wires.start(part, self.from_near.at[1, pl.ds(side, side)], me.x_down))

    def sums(self, part):
        rows = pl.ds(pl.multiple_of(part * 256, 256), 256)
        return [self.held(0).at[rows], self.from_near.at[0, rows], self.from_near.at[1, rows]]

    def start_z(self):
        for copy in self.near:
            copy.wait_recv()
        self.z = []
        for i, (where, part) in enumerate(self.partners):
            sums = self.sums(part)
            add_into(sums[0], *sums)
            self.z.append(self.wires.start(sums[0], self.from_z.at[i], where))

    def wait(self):
        for copy in self.z:
            copy.wait_recv()
        self.all = self.sums(self.part) + [self.from_z.at[i] for i in range(len(self.z))]

    def result(self, rows):
        total = self.all[0][rows, :].astype(jnp.float32)
        for part in self.all[1:]:
            total = total + part[rows, :].astype(jnp.float32)
        return total

    @staticmethod
    def scratch(rows, partners):
        blocks = lambda *shape: pltpu.VMEM(shape, jnp.bfloat16)
        return [
            blocks(4, rows, B),
            blocks(2, rows // 2, B),
            blocks(2, rows, B),
            blocks(partners, 256, B),
        ]


class WeightScatter:
    def __init__(self, me, wires, terms, part, from_far, from_near):
        rows = pl.ds(part * 256, 256)
        self.me, self.wires, self.rows = me, wires, rows
        self.block = lambda j: terms.at[j, rows]
        self.from_far = [from_far.at[i, rows] for i in range(2)]
        self.from_near = lambda i: from_near.at[i, rows]

    def start_far(self):
        me, y = self.me, self.me.ys
        self.far = [
            self.wires.start(self.block(y[2]), self.from_far[0], me.y_up),
            self.wires.start(self.block(4 + y[2]), self.from_far[1], me.y_down),
        ]

    def start_direct(self):
        me, y = self.me, self.me.ys
        self.near = [
            self.wires.start(self.block(4 + y[1]), self.from_near(1), me.y_up),
            self.wires.start(self.block(y[3]), self.from_near(2), me.y_down),
        ]

    def start_near(self):
        me, y = self.me, self.me.ys
        self.far[0].wait_recv()
        block = self.block(y[1])
        add_into(block, block, self.from_far[0])
        self.near.append(self.wires.start(block, self.from_near(0), me.y_up))
        self.far[1].wait_recv()
        block = self.block(4 + y[3])
        add_into(block, block, self.from_far[1])
        self.near.append(self.wires.start(block, self.from_near(3), me.y_down))

    def parts(self, zh):
        return [self.block(zh * 4 + self.me.y), self.from_near(zh), self.from_near(2 + zh)]


    def start_z(self, from_z):
        for copy in self.near:
            copy.wait_recv()
        self.from_z = from_z.at[self.rows]
        other = self.block(self.me.slab(0, 1))
        add_into(other, *self.parts(1 - self.me.zh))
        self.z = self.wires.start(other, self.from_z, self.me.other_zh)

    def start_out(self, out, sem):
        self.z.wait_recv()
        block = self.block(self.me.s)
        add_into(block, *self.parts(self.me.zh), self.from_z)
        self.last = [self.wires.start(block, out, self.me.other_zl)]
        self.here = pltpu.make_async_copy(block, out, sem)
        self.here.start()


    def start_quarters(self, out, sem):
        me = self.me
        for copy in self.near:
            copy.wait_recv()
        mine, other = self.block(me.s), self.block(me.slab(0, 1))
        add_into(other, *self.parts(1 - me.zh))
        self.last = [self.wires.start(other, out, where) for where in (me.other_zh, me.diagonal)]
        add_into(mine, *self.parts(me.zh))
        self.last.append(self.wires.start(mine, out, me.other_zl))
        self.here = pltpu.make_async_copy(mine, out, sem)
        self.here.start()

    def wait_out(self):
        for copy in self.last:
            copy.wait_recv()
        self.here.wait()

    @staticmethod
    def scratch(rows):
        blocks = lambda *shape: pltpu.VMEM(shape, jnp.bfloat16)
        return [blocks(2, rows, B), blocks(4, rows, B)]


class Halo:
    def __init__(self, me, wires, planes, came, field):
        self.me, self.wires, self.planes, self.came, self.field = me, wires, planes, came, field

    def start(self):
        me = self.me
        self.copies = [
            self.wires.start(self.planes.at[1], self.came.at[0], me.y_up),
            self.wires.start(self.planes.at[0], self.came.at[1], me.y_down),
        ]

    def wait(self):
        for copy in self.copies:
            copy.wait_recv()
        low_inside = (self.me.y != 0).astype(jnp.float32)
        high_inside = (self.me.y != 3).astype(jnp.float32)
        for snap in range(2):
            low = [self.came[0, snap * 2 + zh].astype(jnp.float32) for zh in range(2)]
            high = [self.came[1, snap * 2 + zh].astype(jnp.float32) for zh in range(2)]
            edges = [
                (0, 0, low[0] * low_inside),
                (1, 0, low[1] * low_inside + low[0] * (1.0 - low_inside)),
                (0, 5, high[0] * high_inside + high[1] * (1.0 - high_inside)),
                (1, 5, high[1] * high_inside),
            ]
            for zh, place, plane in edges:
                self.field[(snap * 2 + zh) * 6 + place, 1:9] = plane.reshape(8, 8, HID)


def put_rows(part, rows_of, field, planes):
    for p in range(4):
        rounded = rows_of(p).astype(jnp.bfloat16)
        field[part * 6 + 1 + p, 1:9] = rounded.astype(jnp.float32).reshape(8, 8, HID)
        if p in (0, 3):
            planes[p // 3, part] = rounded


def shift(value, by):
    cells = lax.broadcasted_iota(jnp.int32, value.shape, 1)
    moved = pltpu.roll(value, by % 8, 1)
    return jnp.where(cells == (0 if by == 1 else 7), 0.0, moved)


def conv_planes(field, taps, flipped, count, which, finish):
    def body(i):
        part, p = which(i)
        for lane in range(0, HID, 128):
            lanes = pl.ds(lane, 128)
            by_c = [None] * 3
            for a in range(3):
                for b in range(3):
                    window = field[part * 6 + p + a, pl.ds(b, 8), :, lanes]
                    for c in range(3):
                        index = a * 9 + b * 3 + c
                        index = 26 - index if flipped else index
                        term = window * taps[pl.ds(index, 1), lanes].reshape(1, 1, 128)
                        by_c[c] = term if by_c[c] is None else by_c[c] + term
            total = by_c[1] + shift(by_c[0], 1) + shift(by_c[2], -1)
            finish(chunk(part * 4 + p), lanes, total.reshape(CHUNK, 128))

    loop(count, body)


def inner(i):
    return lax.div(i, 2), 1 + lax.rem(i, 2)


def outer(i):
    return lax.div(i, 2), 3 * lax.rem(i, 2)


def gelu_pair(preact):
    inner_value = gelu_scale * (preact + gelu_cubic * preact * preact * preact)
    tangent = jnp.tanh(inner_value)
    value = 0.5 * preact * (1.0 + tangent)
    slope = 0.5 * (1.0 + tangent) + 0.5 * preact * (1.0 - tangent * tangent) * gelu_scale * (
        1.0 + 3.0 * gelu_cubic * preact * preact
    )
    return (value, slope)


def dot(left, right, left_dim, right_dim):
    return lax.dot_general(
        left, right, (((left_dim,), (right_dim,)), ((), ())), preferred_element_type=jnp.float32
    )


def block_kernel(
    tok, gout, gain, up, down, taps_all,
    mixed_out, tokens_out, up_out, down_out, conv_out, gain_out,
    T, G, U, D, N, PB, gains, taps, field, d_field, total, slope, active, d_lifted, inverse,
    lift_here, lift_came, planes, came, d_norm, row_part, conv_sums, conv_terms, row_pair, row_terms,
    gain_z, gain_terms,
    b0, b1, b2, b3, n0, n1, n2, n3, w0, w1, v0, v1, v2,
    local, send, recv,
):
    me = Place()
    meet(me.partners())
    wires = Wires(send, recv)
    hidden = pl.ds(pl.multiple_of(me.zl * B, B), B)
    quarter = pl.ds(pl.multiple_of(me.rb * HID, HID), HID)
    other_quarter = pl.ds(pl.multiple_of((me.zl * 2 + 1 - me.zh) * HID, HID), HID)
    up_own, down_own = up.at[:, hidden], down.at[quarter, :]
    u = WeightGather(me, wires, up_own, up_own, U)
    d = WeightGather(me, wires, down_own, down.at[other_quarter, :], D)
    t = TokenGather(me, wires, tok, T, me.zl, [(me.other_zl, 1 - me.zl)])
    g = TokenGather(me, wires, gout, G, me.rb, me.z_peers)
    PN, GU, GD, d_slabs = N, G, T, lift_here
    b = RowScatter(me, wires, PB, me.rb, me.z_peers, b0, b1, b2, b3)
    n = RowScatter(me, wires, PN, me.zl, [(me.other_zl, 1 - me.zl)], n0, n1, n2, n3)
    gd = WeightScatter(me, wires, GD, 0, w0, w1)
    gus = [WeightScatter(me, wires, GU, part, v0, v1) for part in range(2)]

    t.start_z()
    u.start_z()
    u.start_y()
    t.start(0)
    gain_copies = [wires.start(gain, gains.at[me.f], where) for where in me.x_peers + [me.other_core]]
    here = [
        pltpu.make_async_copy(src, dst, local.at[i])
        for i, (src, dst) in enumerate(
            [
                (tok, T.at[me.f, t.rows(0)]),
                (gain, gains.at[me.f]),
                (up_own, U.at[me.s]),
                (taps_all.at[:, quarter], taps),
                (gout, G.at[me.f, g.rows(0)]),
                (down_own, D.at[me.s]),
            ]
        )
    ]
    for copy in here:
        copy.start()
    field[...] = jnp.zeros_like(field)
    d_field[...] = jnp.zeros_like(d_field)
    t.forward(0)
    t.start(1)
    g.start_z()
    for copy in gain_copies[:3]:
        copy.wait_recv()
    for k in (1, 2, 3):
        block = gains.at[me.feat(k)]
        gain_copies.append(wires.start(block, block, me.other_core))
    u.forward_own()
    u.start_other()
    d.start_z()
    t.finish(0)
    g.start(0)
    t.forward(1)
    d.start_y()
    t.finish(1)
    g.forward(0)
    g.start(1)
    for copy in here:
        copy.wait()
    for copy in gain_copies[3:]:
        copy.wait_recv()
    t.wait_cores()

    def normalise(r):
        rows = chunk(r)
        squares = jnp.zeros((CHUNK, 128), jnp.float32)
        for k in range(8):
            for lane in range(0, B, 128):
                value = T[k, rows, pl.ds(lane, 128)].astype(jnp.float32)
                squares = squares + value * value
        mean = jnp.sum(squares, axis=1, keepdims=True) / 4096.0
        inv = jnp.broadcast_to(lax.rsqrt(mean + epsilon), (CHUNK, 128))
        inverse[rows, :] = inv
        for k in range(8):
            for lane in range(0, B, 128):
                lanes = pl.ds(lane, 128)
                value = T[k, rows, lanes].astype(jnp.float32) * inv * gains[k, 0:1, lanes]
                N[k, rows, lanes] = value.astype(jnp.bfloat16)

    loop(8, normalise)
    total[...] = jnp.zeros_like(total)

    def lift(zh):
        def body(i):
            j = zh * 4 + i
            for half in range(2):
                total[pl.ds(half * B, B), :] += dot(N[j], U[j, :, pl.ds(half * HID, HID)], 1, 0)

        loop(4, body)

    u.wait_far()
    u.forward_other()
    lift(me.zh)
    g.finish(0)
    g.forward(1)
    g.start(2)
    d.forward_own()
    d.start_other()
    u.wait_far_other()
    lift(1 - me.zh)

    def round_lift(r):
        lift_here[chunk(r), :] = total[chunk(r), :].astype(jnp.bfloat16)

    loop(16, round_lift)
    lift_side = lambda zh: lift_here.at[pl.ds(pl.multiple_of(zh * B, B), B)]
    lift_copy = wires.start(lift_side(1 - me.zh), lift_came, me.other_zh)
    g.finish(1)
    g.forward(2)
    g.start(3)
    mine = lift_side(me.zh)
    for snap in range(2):
        put_rows(snap * 2 + me.zh, lambda p: mine[pl.ds(snap * 256 + p * CHUNK, CHUNK), :], field, planes.at[0])
    lift_copy.wait_recv()
    for snap in range(2):
        put_rows(
            snap * 2 + 1 - me.zh, lambda p: lift_came[pl.ds(snap * 256 + p * CHUNK, CHUNK), :], field, planes.at[0]
        )
    halo = Halo(me, wires, planes.at[0], came.at[0], field)
    halo.start()

    def activate(rows, lanes, preact):
        value, rate = gelu_pair(preact)
        active[rows, lanes] = value.astype(jnp.bfloat16)
        slope[rows, lanes] = rate

    conv_planes(field, taps, False, 8, inner, activate)
    d.wait_far()
    d.forward_other()
    halo.wait()
    conv_planes(field, taps, False, 8, outer, activate)
    g.finish(2)
    g.forward(3)
    d.wait_far_other()
    g.finish(3)
    g.wait_cores()
    gathered = len(wires.copies)
    total[...] = jnp.zeros_like(total)

    def d_active(j):
        total[...] += dot(G[j], D[j], 1, 1)

    loop(8, d_active)

    def d_preact(i):
        part = i
        put_rows(
            part,
            lambda p: total[chunk(part * 4 + p), :] * slope[chunk(part * 4 + p), :],
            d_field,
            planes.at[1],
        )

    loop(4, d_preact)
    d_halo = Halo(me, wires, planes.at[1], came.at[1], d_field)
    d_halo.start()

    wires.flush(gathered)

    def down_term(j):
        GD[j, pl.ds(0, HID), :] = dot(active[...], G[j], 0, 0).astype(jnp.bfloat16)

    loop(8, down_term)
    gd.start_far()
    gd.start_direct()

    def d_lift(rows, lanes, value):
        d_slabs[rows, lanes] = value.astype(jnp.bfloat16)

    conv_planes(d_field, taps, True, 8, inner, d_lift)
    d_halo.wait()
    conv_planes(d_field, taps, True, 8, outer, d_lift)
    d_columns = pl.ds(pl.multiple_of(me.zh * HID, HID), HID)
    d_copies = [
        wires.start(
            d_slabs.at[pl.ds(pl.multiple_of((snap * 2 + 1 - me.zh) * 256, 256), 256), :],
            d_lifted.at[pl.ds(snap * 256, 256), d_columns],
            me.other_zh,
        )
        for snap in range(2)
    ]
    for snap in range(2):
        d_lifted[pl.ds(snap * 256, 256), d_columns] = d_slabs[
            pl.ds(pl.multiple_of((snap * 2 + me.zh) * 256, 256), 256), :
        ]

    def branch_term(j):
        PB[j] = dot(active[...], D[j], 1, 0).astype(jnp.bfloat16)

    loop(8, branch_term)
    b.start_core()
    b.start_far()
    for copy in d_copies:
        copy.wait_recv()

    def up_term(j):
        GU[j, pl.ds(0, B), :] = dot(N[j], d_lifted[...], 0, 0).astype(jnp.bfloat16)

    loop(8, up_term)
    for part in gus:
        part.start_far()
    gd.start_near()

    def norm_term(j):
        PN[j] = dot(d_lifted[...], U[j], 1, 1).astype(jnp.bfloat16)

    loop(8, norm_term)
    n.start_core()
    for part in gus:
        part.start_direct()
    b.start_near()
    n.start_far()

    conv_sums[...] = jnp.zeros_like(conv_sums)

    def taps_grad(i):
        part, p = lax.div(i, 4), lax.rem(i, 4)
        for lane in range(0, HID, 128):
            lanes = pl.ds(lane, 128)
            here_d = d_field[part * 6 + 1 + p, pl.ds(1, 8), :, lanes]
            by_c = [shift(here_d, -1), here_d, shift(here_d, 1)]
            for a in range(3):
                for b_ in range(3):
                    window = field[part * 6 + p + a, pl.ds(b_, 8), :, lanes]
                    for c in range(3):
                        term = jnp.sum(by_c[c] * window, axis=0)
                        conv_sums[a * 9 + b_ * 3 + c, :, lanes] += term

    loop(16, taps_grad)
    conv_terms[me.y] = jnp.sum(conv_sums[...], axis=1).astype(jnp.bfloat16)
    conv_copies = [wires.start(conv_terms.at[me.y], conv_terms.at[me.y], where) for where in me.y_peers]

    gd.start_quarters(down_out.at[quarter, :], local.at[0])
    gus[0].start_near()
    gus[1].start_near()
    b.start_z()
    n.start_near()
    b.wait()

    def mix(r):
        rows = chunk(r)
        mixed_out[rows, :] = (tok[rows, :].astype(jnp.float32) + b.result(rows)).astype(jnp.bfloat16)

    loop(4, mix)
    for copy in conv_copies:
        copy.wait_recv()
    conv = conv_terms[0].astype(jnp.float32)
    for k in range(1, 4):
        conv = conv + conv_terms[k].astype(jnp.float32)
    conv_out[me.rb] = conv
    last_copies = [wires.start(conv_out.at[me.rb], conv_out.at[me.rb], where) for where, _ in me.z_peers]
    gus[0].start_z(v2)
    n.start_z()
    n.wait()

    def rows_part(r, gain_sum):
        rows = chunk(r)
        whole = n.result(rows)
        d_norm[rows, :] = whole
        inv = inverse[chunk(r, me.zl * 256), :]
        part = jnp.zeros((CHUNK, 128), jnp.float32)
        sums = []
        for lane in range(0, B, 128):
            lanes = slice(lane, lane + 128)
            with_hat = whole[:, lanes] * (tok[rows, lanes].astype(jnp.float32) * inv)
            part = part + with_hat * gain[0:1, lanes]
            sums.append(jnp.sum(with_hat.reshape(8, 8, 128), axis=0))
        row_part[rows, :] = part
        return gain_sum + jnp.concatenate(sums, axis=1)

    gain_sum = lax.fori_loop(0, 4, rows_part, jnp.zeros((8, B), jnp.float32))
    row_sum = jnp.sum(jnp.transpose(row_part[...]), axis=0, keepdims=True)
    row_pair[me.c] = jnp.broadcast_to(row_sum, (8, 256))
    row_copy = wires.start(row_pair.at[me.c], row_pair.at[me.c], me.other_core)
    gain_z[me.rb] = jnp.broadcast_to(jnp.sum(gain_sum, axis=0, keepdims=True), (8, B))
    gain_copies = [wires.start(gain_z.at[me.rb], gain_z.at[me.rb], where) for where, _ in me.z_peers]
    row_copy.wait_recv()
    row_terms[me.x] = row_pair[0] + row_pair[1]
    row_copies = [wires.start(row_terms.at[me.x], row_terms.at[me.x], where) for where in me.x_peers]
    gus[1].start_z(v2)
    for copy in gain_copies:
        copy.wait_recv()
    gain_terms[me.y] = (gain_z[0] + gain_z[1]) + (gain_z[2] + gain_z[3])
    last_copies += [wires.start(gain_terms.at[me.y], gain_terms.at[me.y], where) for where in me.y_peers]
    for copy in row_copies:
        copy.wait_recv()
    rows_sum = (row_terms[0] + row_terms[1]) + (row_terms[2] + row_terms[3])
    row_part[...] = jnp.transpose(jnp.broadcast_to(rows_sum[0:1, :], (128, 256)))
    gus[0].start_out(up_out.at[pl.ds(0, 256), hidden], local.at[1])

    def finish(r):
        rows = chunk(r)
        inv = inverse[chunk(r, me.zl * 256), :]
        share = row_part[rows, :] / 4096.0
        for lane in range(0, B, 128):
            lanes = slice(lane, lane + 128)
            hat = tok[rows, lanes].astype(jnp.float32) * inv
            value = inv * (d_norm[rows, lanes] * gain[0:1, lanes] - hat * share)
            tokens_out[rows, lanes] = (gout[rows, lanes].astype(jnp.float32) + value).astype(jnp.bfloat16)

    loop(4, finish)
    gus[1].start_out(up_out.at[pl.ds(256, 256), hidden], local.at[2])
    for copy in last_copies:
        copy.wait_recv()
    gain_out[...] = (gain_terms[0] + gain_terms[1]) + (gain_terms[2] + gain_terms[3])
    for part in [gd] + gus:
        part.wait_out()
    wires.flush()


def block(tok, gout, gain, up, down, taps):
    vmem = pl.BlockSpec(memory_space=pltpu.VMEM)
    anywhere = pl.BlockSpec(memory_space=pl.ANY)
    bf16, f32 = jnp.bfloat16, jnp.float32
    blocks = lambda *shape: pltpu.VMEM(shape, bf16)
    floats = lambda *shape: pltpu.VMEM(shape, f32)
    return pl.pallas_call(
        block_kernel,
        out_shape=[
            jax.ShapeDtypeStruct((256, B), bf16),
            jax.ShapeDtypeStruct((256, B), bf16),
            jax.ShapeDtypeStruct((B, 2 * B), bf16),
            jax.ShapeDtypeStruct((2 * B, B), bf16),
            jax.ShapeDtypeStruct((4, 32, HID), f32),
            jax.ShapeDtypeStruct((8, B), f32),
        ],
        in_specs=[vmem, vmem, vmem, anywhere, anywhere, anywhere],
        out_specs=[vmem, vmem, anywhere, anywhere, vmem, vmem],
        scratch_shapes=[
            blocks(8, B, B),
            blocks(8, 2 * B, B),
            blocks(8, B, B),
            blocks(8, HID, B),
            blocks(8, B, B),
            blocks(8, 2 * B, B),
            floats(8, 8, B),
            floats(27, HID),
            floats(24, 10, 8, HID),
            floats(24, 10, 8, HID),
            floats(2 * B, HID),
            floats(2 * B, HID),
            blocks(2 * B, HID),
            blocks(B, B),
            floats(B, 128),
            blocks(2 * B, HID),
            blocks(B, HID),
            blocks(2, 2, 4, CHUNK, HID),
            blocks(2, 2, 4, CHUNK, HID),
            floats(256, B),
            floats(256, 128),
            floats(32, 8, HID),
            blocks(4, 32, HID),
            floats(2, 8, 256),
            floats(4, 8, 256),
            floats(4, 8, B),
            floats(4, 8, B),
        ]
        + RowScatter.scratch(2 * B, 3)
        + RowScatter.scratch(B, 1)
        + WeightScatter.scratch(HID)
        + WeightScatter.scratch(B)
        + [blocks(B, B)]
        + [pltpu.SemaphoreType.DMA((6,)), pltpu.SemaphoreType.DMA((176,)), pltpu.SemaphoreType.DMA((176,))],
        compiler_params=pltpu.CompilerParams(
            collective_id=0, has_side_effects=True, vmem_limit_bytes=62 << 20
        ),
        name="block",
    )(tok, gout, gain, up, down, taps)


def per_device(tokens, grad_out, gain, up_weight, down_weight, conv_taps):
    tok = tokens.reshape(256, B)
    gout = grad_out.reshape(256, B)
    gain_rows = jnp.broadcast_to(gain[None], (8, B))
    mixed, grad_tokens, grad_up, grad_down, conv, last = block(
        tok, gout, gain_rows, up_weight, down_weight, conv_taps
    )
    grad_conv = conv[:, :27].transpose(1, 0, 2).reshape(27, 2 * B)
    return (
        mixed.reshape(tokens.shape),
        grad_tokens.reshape(tokens.shape),
        grad_up,
        grad_down,
        grad_conv,
        last[0],
    )


def solution(mesh):
    rows = P("dp", "seq", None, None, "fsdp")
    return jax.shard_map(
        per_device,
        mesh=mesh,
        in_specs=(rows, rows, P("fsdp"), P("seq", "fsdp"), P("fsdp", "seq"), P(None, "fsdp")),
        out_specs=(rows, rows, P("seq", "fsdp"), P("fsdp", "seq"), P(None, "fsdp"), P("fsdp")),
        check_vma=False,
    )
```

```python
import jax
import jax.numpy as jnp
from jax import lax
from jax.experimental import pallas as pl
from jax.experimental.pallas import tpu as pltpu
from jax.sharding import PartitionSpec as P

MESH = pl.DeviceIdType.MESH
gelu_scale = 0.7978845608028654
gelu_cubic = 0.044715
epsilon = 1e-06
B = 512


class Place:
    def __init__(self):
        self.zl = lax.axis_index("dp")
        self.f = lax.axis_index("fsdp")
        self.s = lax.axis_index("seq")
        self.x, self.c = lax.div(self.f, 2), lax.rem(self.f, 2)
        self.zh, self.y = lax.div(self.s, 4), lax.rem(self.s, 4)
        self.xs = [lax.rem(self.x + k, 4) for k in range(4)]
        self.ys = [lax.rem(self.y + k, 4) for k in range(4)]
        self.other_zl = {"dp": 1 - self.zl}
        self.other_core = {"fsdp": self.feat(0, 1)}
        self.x_up, self.x_down = {"fsdp": self.feat(1)}, {"fsdp": self.feat(3)}
        self.other_zh = {"seq": self.slab(0, 1)}
        self.y_up, self.y_down = {"seq": self.slab(1)}, {"seq": self.slab(3)}
        self.x_far, self.y_far = {"fsdp": self.feat(2)}, {"seq": self.slab(2)}
        self.diagonal = {"dp": 1 - self.zl, "seq": self.slab(0, 1)}
        self.rb = self.zl * 2 + self.zh
        self.z_peers = [
            (self.other_zl, (1 - self.zl) * 2 + self.zh),
            (self.other_zh, self.zl * 2 + 1 - self.zh),
            (self.diagonal, 3 - self.rb),
        ]
        self.x_peers = [self.x_up, self.x_far, self.x_down]
        self.y_peers = [self.y_up, self.y_far, self.y_down]

    def feat(self, k, flip=0):
        return self.xs[k] * 2 + (1 - self.c if flip else self.c)

    def slab(self, k, flip=0):
        return (1 - self.zh if flip else self.zh) * 4 + self.ys[k]

    def partners(self):
        return self.x_peers + self.y_peers + [where for where, _ in self.z_peers] + [self.other_core]


class Wires:
    def __init__(self, send, recv):
        self.send, self.recv, self.copies, self.left = send, recv, [], 0

    def start(self, src, dst, where):
        i = len(self.copies)
        copy = pltpu.make_async_remote_copy(
            src_ref=src, dst_ref=dst, send_sem=self.send.at[i], recv_sem=self.recv.at[i],
            device_id=where, device_id_type=MESH,
        )
        copy.start()
        self.copies.append(copy)
        return copy

    def flush(self, until=None):
        for copy in self.copies[self.left : until]:
            copy.wait_send()
        self.left = len(self.copies) if until is None else until


def meet(partners):
    barrier = pltpu.get_barrier_semaphore()
    for where in partners:
        pl.semaphore_signal(barrier, inc=1, device_id=where, device_id_type=MESH)
    pl.semaphore_wait(barrier, len(partners))


class WeightGather:
    def __init__(self, me, wires, own, for_other, buf):
        self.me, self.wires, self.own, self.for_other, self.buf = me, wires, own, for_other, buf
        self.half = buf.shape[1] // 2

    def start_z(self):
        self.z = self.wires.start(self.for_other, self.buf.at[self.me.s], self.me.other_zh)

    def start_y(self):
        self.up = self.wires.start(self.own, self.buf.at[self.me.s], self.me.y_up)
        self.down = self.wires.start(self.own, self.buf.at[self.me.s], self.me.y_down)

    def forward(self, flip):
        me, buf = self.me, self.buf
        below, above = me.slab(3, flip), me.slab(1, flip)
        self.up.wait_recv()
        part = buf.at[below, pl.ds(0, self.half)]
        first = self.wires.start(part, part, me.y_up)
        self.down.wait_recv()
        part = buf.at[above, pl.ds(self.half, self.half)]
        return first, self.wires.start(part, part, me.y_down)

    def forward_own(self):
        self.far = self.forward(0)

    def start_other(self):
        self.z.wait_recv()
        block = self.buf.at[self.me.slab(0, 1)]
        self.up = self.wires.start(block, block, self.me.y_up)
        self.down = self.wires.start(block, block, self.me.y_down)

    def forward_other(self):
        self.far_other = self.forward(1)

    def wait_far(self):
        for copy in self.far:
            copy.wait_recv()

    def wait_far_other(self):
        for copy in self.far_other:
            copy.wait_recv()


class TokenGather:
    def __init__(self, me, wires, own, buf, part, partners):
        self.me, self.wires, self.own, self.buf = me, wires, own, buf
        self.partners = [where for where, _ in partners]
        self.parts = [part] + [place for _, place in partners]
        self.ring, self.far, self.cores = {}, {}, []

    def rows(self, i, half=None):
        if half is None:
            return pl.ds(pl.multiple_of(self.parts[i] * 256, 256), 256)
        return pl.ds(pl.multiple_of(self.parts[i] * 256 + half * 128, 128), 128)

    def start_z(self):
        dst = self.buf.at[self.me.f, self.rows(0)]
        self.z = [self.wires.start(self.own, dst, where) for where in self.partners]

    def start(self, i):
        me = self.me
        dst = self.buf.at[me.f, self.rows(i)]
        src = dst if i else self.own
        if i:
            self.z[i - 1].wait_recv()
        self.ring[i] = [self.wires.start(src, dst, where) for where in (me.x_up, me.x_down)]
        self.cores.append(self.wires.start(src, dst, me.other_core))

    def to_core(self, k, i):
        block = self.buf.at[self.me.feat(k), self.rows(i)]
        self.cores.append(self.wires.start(block, block, self.me.other_core))

    def forward(self, i):
        me, buf = self.me, self.buf
        self.ring[i][0].wait_recv()
        part = buf.at[me.feat(3), self.rows(i, 0)]
        first = self.wires.start(part, part, me.x_up)
        self.ring[i][1].wait_recv()
        part = buf.at[me.feat(1), self.rows(i, 1)]
        self.far[i] = first, self.wires.start(part, part, me.x_down)
        self.to_core(3, i)
        self.to_core(1, i)

    def finish(self, i):
        for copy in self.far[i]:
            copy.wait_recv()
        self.to_core(2, i)

    def wait_cores(self):
        for copy in self.cores:
            copy.wait_recv()


CHUNK = 64
HID = 256


def chunk(r, base=0):
    return pl.ds(pl.multiple_of(base + r * CHUNK, CHUNK), CHUNK)


def loop(count, body):
    def step(i, carry):
        body(i)
        return carry

    lax.fori_loop(0, count, step, 0)


def add_into(dst, *parts):
    def body(r):
        rows = chunk(r)
        total = parts[0][rows, :].astype(jnp.float32)
        for part in parts[1:]:
            total = total + part[rows, :].astype(jnp.float32)
        dst[rows, :] = total.astype(dst.dtype)

    loop(dst.shape[0] // CHUNK, body)


class RowScatter:
    def __init__(self, me, wires, terms, part, partners, from_core, from_far, from_near, from_z):
        self.me, self.wires, self.terms = me, wires, terms
        self.part, self.partners = part, partners
        self.from_core, self.from_far, self.from_near = from_core, from_far, from_near
        self.from_z = from_z
        self.side = terms.shape[1] // 2

    def start_core(self):
        me = self.me
        self.core = {}
        for k in (2, 1, 3, 0):
            self.core[k] = self.wires.start(
                self.terms.at[me.feat(k, 1)], self.from_core.at[me.xs[k]], me.other_core
            )

    def held(self, k):
        return self.terms.at[self.me.feat(k)]

    def join(self, k):
        self.core[k].wait_recv()
        add_into(self.held(k), self.held(k), self.from_core.at[self.me.xs[k]])

    def start_far(self):
        me, side = self.me, self.side
        self.join(2)
        self.far = [
            self.wires.start(self.held(2).at[pl.ds(0, side)], self.from_far.at[0], me.x_up),
            self.wires.start(self.held(2).at[pl.ds(side, side)], self.from_far.at[1], me.x_down),
        ]
        self.join(1)
        self.join(3)
        self.near = [
            self.wires.start(self.held(1).at[pl.ds(side, side)], self.from_near.at[0, pl.ds(side, side)], me.x_up),
            self.wires.start(self.held(3).at[pl.ds(0, side)], self.from_near.at[1, pl.ds(0, side)], me.x_down),
        ]
        self.join(0)

    def start_near(self):
        me, side = self.me, self.side
        self.far[0].wait_recv()
        part = self.held(1).at[pl.ds(0, side)]
        add_into(part, part, self.from_far.at[0])
        self.near.append(self.wires.start(part, self.from_near.at[0, pl.ds(0, side)], me.x_up))
        self.far[1].wait_recv()
        part = self.held(3).at[pl.ds(side, side)]
        add_into(part, part, self.from_far.at[1])
        self.near.append(self.wires.start(part, self.from_near.at[1, pl.ds(side, side)], me.x_down))

    def sums(self, part):
        rows = pl.ds(pl.multiple_of(part * 256, 256), 256)
        return [self.held(0).at[rows], self.from_near.at[0, rows], self.from_near.at[1, rows]]

    def start_z(self):
        for copy in self.near:
            copy.wait_recv()
        self.z = []
        for i, (where, part) in enumerate(self.partners):
            sums = self.sums(part)
            add_into(sums[0], *sums)
            self.z.append(self.wires.start(sums[0], self.from_z.at[i], where))

    def wait(self):
        for copy in self.z:
            copy.wait_recv()
        self.all = self.sums(self.part) + [self.from_z.at[i] for i in range(len(self.z))]

    def result(self, rows):
        total = self.all[0][rows, :].astype(jnp.float32)
        for part in self.all[1:]:
            total = total + part[rows, :].astype(jnp.float32)
        return total

    @staticmethod
    def scratch(rows, partners):
        blocks = lambda *shape: pltpu.VMEM(shape, jnp.bfloat16)
        return [
            blocks(4, rows, B),
            blocks(2, rows // 2, B),
            blocks(2, rows, B),
            blocks(partners, 256, B),
        ]


class WeightScatter:
    def __init__(self, me, wires, terms, start, size, from_far, from_near):
        rows = pl.ds(start, size)
        self.me, self.wires, self.rows = me, wires, rows
        self.block = lambda j: terms.at[j, rows]
        self.from_far = [from_far.at[i, rows] for i in range(2)]
        self.from_near = lambda i: from_near.at[i, rows]

    def start_far(self):
        me, y = self.me, self.me.ys
        self.far = [
            self.wires.start(self.block(y[2]), self.from_far[0], me.y_up),
            self.wires.start(self.block(4 + y[2]), self.from_far[1], me.y_down),
        ]

    def start_direct(self):
        me, y = self.me, self.me.ys
        self.near = [
            self.wires.start(self.block(4 + y[1]), self.from_near(1), me.y_up),
            self.wires.start(self.block(y[3]), self.from_near(2), me.y_down),
        ]

    def start_near(self):
        me, y = self.me, self.me.ys
        self.far[0].wait_recv()
        block = self.block(y[1])
        add_into(block, block, self.from_far[0])
        self.near.append(self.wires.start(block, self.from_near(0), me.y_up))
        self.far[1].wait_recv()
        block = self.block(4 + y[3])
        add_into(block, block, self.from_far[1])
        self.near.append(self.wires.start(block, self.from_near(3), me.y_down))

    def parts(self, zh):
        return [self.block(zh * 4 + self.me.y), self.from_near(zh), self.from_near(2 + zh)]


    def start_z(self, from_z):
        for copy in self.near:
            copy.wait_recv()
        self.from_z = from_z.at[self.rows]
        other = self.block(self.me.slab(0, 1))
        add_into(other, *self.parts(1 - self.me.zh))
        self.z = self.wires.start(other, self.from_z, self.me.other_zh)

    def start_out(self, out, sem):
        self.z.wait_recv()
        block = self.block(self.me.s)
        add_into(block, *self.parts(self.me.zh), self.from_z)
        self.last = [self.wires.start(block, out, self.me.other_zl)]
        self.here = pltpu.make_async_copy(block, out, sem)
        self.here.start()


    def start_quarters(self, out, sem):
        me = self.me
        for copy in self.near:
            copy.wait_recv()
        mine, other = self.block(me.s), self.block(me.slab(0, 1))
        add_into(other, *self.parts(1 - me.zh))
        self.last = [self.wires.start(other, out, where) for where in (me.other_zh, me.diagonal)]
        add_into(mine, *self.parts(me.zh))
        self.last.append(self.wires.start(mine, out, me.other_zl))
        self.here = pltpu.make_async_copy(mine, out, sem)
        self.here.start()

    def wait_out(self):
        for copy in self.last:
            copy.wait_recv()
        self.here.wait()

    @staticmethod
    def scratch(rows):
        blocks = lambda *shape: pltpu.VMEM(shape, jnp.bfloat16)
        return [blocks(2, rows, B), blocks(4, rows, B)]


class Halo:
    def __init__(self, me, wires, planes, came, field):
        self.me, self.wires, self.planes, self.came, self.field = me, wires, planes, came, field

    def start(self):
        me = self.me
        self.copies = [
            self.wires.start(self.planes.at[1], self.came.at[0], me.y_up),
            self.wires.start(self.planes.at[0], self.came.at[1], me.y_down),
        ]

    def wait(self):
        for copy in self.copies:
            copy.wait_recv()
        low_inside = (self.me.y != 0).astype(jnp.float32)
        high_inside = (self.me.y != 3).astype(jnp.float32)
        for snap in range(2):
            low = [self.came[0, snap * 2 + zh].astype(jnp.float32) for zh in range(2)]
            high = [self.came[1, snap * 2 + zh].astype(jnp.float32) for zh in range(2)]
            edges = [
                (0, 0, low[0] * low_inside),
                (1, 0, low[1] * low_inside + low[0] * (1.0 - low_inside)),
                (0, 5, high[0] * high_inside + high[1] * (1.0 - high_inside)),
                (1, 5, high[1] * high_inside),
            ]
            for zh, place, plane in edges:
                self.field[(snap * 2 + zh) * 6 + place, 1:9] = plane.reshape(8, 8, HID)


def put_rows(part, rows_of, field, planes):
    for p in range(4):
        rounded = rows_of(p).astype(jnp.bfloat16)
        field[part * 6 + 1 + p, 1:9] = rounded.astype(jnp.float32).reshape(8, 8, HID)
        if p in (0, 3):
            planes[p // 3, part] = rounded


def shift(value, by):
    cells = lax.broadcasted_iota(jnp.int32, value.shape, 1)
    moved = pltpu.roll(value, by % 8, 1)
    return jnp.where(cells == (0 if by == 1 else 7), 0.0, moved)


def conv_planes(field, taps, flipped, count, which, finish):
    def body(i):
        part, p = which(i)
        for lane in range(0, HID, 128):
            lanes = pl.ds(lane, 128)
            by_c = [None] * 3
            for a in range(3):
                for b in range(3):
                    window = field[part * 6 + p + a, pl.ds(b, 8), :, lanes]
                    for c in range(3):
                        index = a * 9 + b * 3 + c
                        index = 26 - index if flipped else index
                        term = window * taps[pl.ds(index, 1), lanes].reshape(1, 1, 128)
                        by_c[c] = term if by_c[c] is None else by_c[c] + term
            total = by_c[1] + shift(by_c[0], 1) + shift(by_c[2], -1)
            finish(chunk(part * 4 + p), lanes, total.reshape(CHUNK, 128))

    loop(count, body)


def inner(i):
    return lax.div(i, 2), 1 + lax.rem(i, 2)


def outer(i):
    return lax.div(i, 2), 3 * lax.rem(i, 2)


def gelu_pair(preact):
    inner_value = gelu_scale * (preact + gelu_cubic * preact * preact * preact)
    tangent = jnp.tanh(inner_value)
    value = 0.5 * preact * (1.0 + tangent)
    slope = 0.5 * (1.0 + tangent) + 0.5 * preact * (1.0 - tangent * tangent) * gelu_scale * (
        1.0 + 3.0 * gelu_cubic * preact * preact
    )
    return (value, slope)


def dot(left, right, left_dim, right_dim):
    return lax.dot_general(
        left, right, (((left_dim,), (right_dim,)), ((), ())), preferred_element_type=jnp.float32
    )


def block_kernel(
    tok, gout, gain, up, down, taps_all,
    mixed_out, tokens_out, up_out, down_out, conv_out, gain_out,
    T, G, U, D, N, PB, gains, taps, field, d_field, total, slope, active, d_lifted, inverse,
    lift_here, lift_came, planes, came, d_norm, row_part, conv_sums, conv_terms, row_pair, row_terms,
    gain_z, gain_terms,
    b0, b1, b2, b3, n0, n1, n2, n3, w0, w1, v0, v1, v2,
    local, send, recv,
):
    me = Place()
    meet(me.partners())
    wires = Wires(send, recv)
    hidden = pl.ds(pl.multiple_of(me.zl * B, B), B)
    quarter = pl.ds(pl.multiple_of(me.rb * HID, HID), HID)
    other_quarter = pl.ds(pl.multiple_of((me.zl * 2 + 1 - me.zh) * HID, HID), HID)
    up_own, down_own = up.at[:, hidden], down.at[quarter, :]
    u = WeightGather(me, wires, up_own, up_own, U)
    d = WeightGather(me, wires, down_own, down.at[other_quarter, :], D)
    t = TokenGather(me, wires, tok, T, me.zl, [(me.other_zl, 1 - me.zl)])
    g = TokenGather(me, wires, gout, G, me.rb, me.z_peers)
    PN, GU, GD, d_slabs = N, G, T, lift_here
    b = RowScatter(me, wires, PB, me.rb, me.z_peers, b0, b1, b2, b3)
    n = RowScatter(me, wires, PN, me.zl, [(me.other_zl, 1 - me.zl)], n0, n1, n2, n3)
    gd = WeightScatter(me, wires, GD, 0, HID, w0, w1)
    gus = [WeightScatter(me, wires, GU, i * 128, 128, v0, v1) for i in range(4)]

    t.start_z()
    u.start_y()
    t.start(0)
    gain_copies = [wires.start(gain, gains.at[me.f], where) for where in me.x_peers + [me.other_core]]
    here = [
        pltpu.make_async_copy(src, dst, local.at[i])
        for i, (src, dst) in enumerate(
            [
                (tok, T.at[me.f, t.rows(0)]),
                (gain, gains.at[me.f]),
                (up_own, U.at[me.s]),
                (taps_all.at[:, quarter], taps),
                (gout, G.at[me.f, g.rows(0)]),
                (down_own, D.at[me.s]),
            ]
        )
    ]
    for copy in here:
        copy.start()
    u.start_z()
    g.start(0)
    field[...] = jnp.zeros_like(field)
    d_field[...] = jnp.zeros_like(d_field)
    t.forward(0)
    t.start(1)
    g.start_z()
    for copy in gain_copies[:3]:
        copy.wait_recv()
    for k in (1, 2, 3):
        block = gains.at[me.feat(k)]
        gain_copies.append(wires.start(block, block, me.other_core))
    u.forward_own()
    t.finish(0)
    g.forward(0)
    t.forward(1)
    u.start_other()
    d.start_z()
    g.start(1)
    t.finish(1)
    d.start_y()
    g.start(2)
    for copy in here:
        copy.wait()
    for copy in gain_copies[3:]:
        copy.wait_recv()
    t.wait_cores()

    def normalise(r):
        rows = chunk(r)
        squares = jnp.zeros((CHUNK, 128), jnp.float32)
        for k in range(8):
            for lane in range(0, B, 128):
                value = T[k, rows, pl.ds(lane, 128)].astype(jnp.float32)
                squares = squares + value * value
        mean = jnp.sum(squares, axis=1, keepdims=True) / 4096.0
        inv = jnp.broadcast_to(lax.rsqrt(mean + epsilon), (CHUNK, 128))
        inverse[rows, :] = inv
        for k in range(8):
            for lane in range(0, B, 128):
                lanes = pl.ds(lane, 128)
                value = T[k, rows, lanes].astype(jnp.float32) * inv * gains[k, 0:1, lanes]
                N[k, rows, lanes] = value.astype(jnp.bfloat16)

    loop(8, normalise)
    total[...] = jnp.zeros_like(total)

    def lift(zh):
        def body(i):
            j = zh * 4 + i
            for half in range(2):
                total[pl.ds(half * B, B), :] += dot(N[j], U[j, :, pl.ds(half * HID, HID)], 1, 0)

        loop(4, body)

    u.wait_far()
    u.forward_other()
    g.finish(0)
    g.forward(1)
    g.start(3)
    lift(me.zh)
    d.forward_own()
    d.start_other()
    u.wait_far_other()
    lift(1 - me.zh)

    def round_lift(r):
        lift_here[chunk(r), :] = total[chunk(r), :].astype(jnp.bfloat16)

    loop(16, round_lift)
    lift_side = lambda zh: lift_here.at[pl.ds(pl.multiple_of(zh * B, B), B)]
    lift_copy = wires.start(lift_side(1 - me.zh), lift_came, me.other_zh)
    g.finish(1)
    g.forward(2)
    mine = lift_side(me.zh)
    for snap in range(2):
        put_rows(snap * 2 + me.zh, lambda p: mine[pl.ds(snap * 256 + p * CHUNK, CHUNK), :], field, planes.at[0])
    lift_copy.wait_recv()
    for snap in range(2):
        put_rows(
            snap * 2 + 1 - me.zh, lambda p: lift_came[pl.ds(snap * 256 + p * CHUNK, CHUNK), :], field, planes.at[0]
        )
    halo = Halo(me, wires, planes.at[0], came.at[0], field)
    halo.start()

    def activate(rows, lanes, preact):
        value, rate = gelu_pair(preact)
        active[rows, lanes] = value.astype(jnp.bfloat16)
        slope[rows, lanes] = rate

    conv_planes(field, taps, False, 8, inner, activate)
    d.wait_far()
    d.forward_other()
    halo.wait()
    conv_planes(field, taps, False, 8, outer, activate)
    g.finish(2)
    g.forward(3)
    d.wait_far_other()

    def branch_term(j):
        PB[j] = dot(active[...], D[j], 1, 0).astype(jnp.bfloat16)

    loop(8, branch_term)
    b.start_core()
    g.finish(3)
    g.wait_cores()
    gathered = len(wires.copies)
    total[...] = jnp.zeros_like(total)

    def d_active(j):
        total[...] += dot(G[j], D[j], 1, 1)

    loop(8, d_active)

    def d_preact(i):
        part = i
        put_rows(
            part,
            lambda p: total[chunk(part * 4 + p), :] * slope[chunk(part * 4 + p), :],
            d_field,
            planes.at[1],
        )

    loop(4, d_preact)
    d_halo = Halo(me, wires, planes.at[1], came.at[1], d_field)
    d_halo.start()

    b.start_far()
    wires.flush(gathered)

    def down_term(j):
        GD[j, pl.ds(0, HID), :] = dot(active[...], G[j], 0, 0).astype(jnp.bfloat16)

    loop(8, down_term)
    gd.start_far()
    gd.start_direct()

    def d_lift(rows, lanes, value):
        d_slabs[rows, lanes] = value.astype(jnp.bfloat16)

    conv_planes(d_field, taps, True, 8, inner, d_lift)
    d_halo.wait()
    conv_planes(d_field, taps, True, 8, outer, d_lift)
    d_columns = pl.ds(pl.multiple_of(me.zh * HID, HID), HID)
    d_copies = [
        wires.start(
            d_slabs.at[pl.ds(pl.multiple_of((snap * 2 + 1 - me.zh) * 256, 256), 256), :],
            d_lifted.at[pl.ds(snap * 256, 256), d_columns],
            me.other_zh,
        )
        for snap in range(2)
    ]
    for snap in range(2):
        d_lifted[pl.ds(snap * 256, 256), d_columns] = d_slabs[
            pl.ds(pl.multiple_of((snap * 2 + me.zh) * 256, 256), 256), :
        ]
    for copy in d_copies:
        copy.wait_recv()
    b.start_near()
    gd.start_near()

    def up_term(j):
        GU[j, pl.ds(0, B), :] = dot(N[j], d_lifted[...], 0, 0).astype(jnp.bfloat16)

    loop(8, up_term)
    for part in gus:
        part.start_far()

    def norm_term(j):
        PN[j] = dot(d_lifted[...], U[j], 1, 1).astype(jnp.bfloat16)

    loop(8, norm_term)
    n.start_core()
    n.start_far()

    conv_sums[...] = jnp.zeros_like(conv_sums)

    def taps_grad(i):
        part, p = lax.div(i, 4), lax.rem(i, 4)
        for lane in range(0, HID, 128):
            lanes = pl.ds(lane, 128)
            here_d = d_field[part * 6 + 1 + p, pl.ds(1, 8), :, lanes]
            by_c = [shift(here_d, -1), here_d, shift(here_d, 1)]
            for a in range(3):
                for b_ in range(3):
                    window = field[part * 6 + p + a, pl.ds(b_, 8), :, lanes]
                    for c in range(3):
                        term = jnp.sum(by_c[c] * window, axis=0)
                        conv_sums[a * 9 + b_ * 3 + c, :, lanes] += term

    loop(16, taps_grad)
    conv_terms[me.y] = jnp.sum(conv_sums[...], axis=1).astype(jnp.bfloat16)
    conv_copies = [wires.start(conv_terms.at[me.y], conv_terms.at[me.y], where) for where in me.y_peers]

    gd.start_quarters(down_out.at[quarter, :], local.at[0])
    for part in gus[:2]:
        part.start_direct()
        part.start_near()
    n.start_near()
    for copy in conv_copies:
        copy.wait_recv()
    conv = conv_terms[0].astype(jnp.float32)
    for k in range(1, 4):
        conv = conv + conv_terms[k].astype(jnp.float32)
    conv_here = conv_out.at[:, quarter]
    conv_here[...] = conv
    last_copies = [wires.start(conv_here, conv_here, where) for where, _ in me.z_peers]
    gus[0].start_z(v2)
    gus[2].start_direct()
    gus[2].start_near()
    b.start_z()
    gus[1].start_z(v2)
    gus[3].start_direct()
    gus[3].start_near()
    n.start_z()
    up_rows = lambda i: up_out.at[pl.ds(i * 128, 128), hidden]
    gus[0].start_out(up_rows(0), local.at[1])
    n.wait()

    def rows_part(r, gain_sum):
        rows = chunk(r)
        whole = n.result(rows)
        d_norm[rows, :] = whole
        inv = inverse[chunk(r, me.zl * 256), :]
        part = jnp.zeros((CHUNK, 128), jnp.float32)
        sums = []
        for lane in range(0, B, 128):
            lanes = slice(lane, lane + 128)
            with_hat = whole[:, lanes] * (tok[rows, lanes].astype(jnp.float32) * inv)
            part = part + with_hat * gain[0:1, lanes]
            sums.append(jnp.sum(with_hat.reshape(8, 8, 128), axis=0))
        row_part[rows, :] = part
        return gain_sum + jnp.concatenate(sums, axis=1)

    gain_sum = lax.fori_loop(0, 4, rows_part, jnp.zeros((8, B), jnp.float32))
    row_sum = jnp.sum(jnp.transpose(row_part[...]), axis=0, keepdims=True)
    row_pair[me.c] = jnp.broadcast_to(row_sum, (8, 256))
    row_copy = wires.start(row_pair.at[me.c], row_pair.at[me.c], me.other_core)
    gain_z[me.rb] = jnp.broadcast_to(jnp.sum(gain_sum, axis=0, keepdims=True), (8, B))
    gain_copies = [wires.start(gain_z.at[me.rb], gain_z.at[me.rb], where) for where, _ in me.z_peers]
    row_copy.wait_recv()
    row_terms[me.x] = row_pair[0] + row_pair[1]
    row_copies = [wires.start(row_terms.at[me.x], row_terms.at[me.x], where) for where in me.x_peers]
    gus[2].start_z(v2)
    gus[1].start_out(up_rows(1), local.at[2])
    for copy in gain_copies:
        copy.wait_recv()
    gain_terms[me.y] = (gain_z[0] + gain_z[1]) + (gain_z[2] + gain_z[3])
    last_copies += [wires.start(gain_terms.at[me.y], gain_terms.at[me.y], where) for where in me.y_peers]
    for copy in row_copies:
        copy.wait_recv()
    rows_sum = (row_terms[0] + row_terms[1]) + (row_terms[2] + row_terms[3])
    row_part[...] = jnp.transpose(jnp.broadcast_to(rows_sum[0:1, :], (128, 256)))
    gus[3].start_z(v2)
    gus[2].start_out(up_rows(2), local.at[3])

    def finish(r):
        rows = chunk(r)
        inv = inverse[chunk(r, me.zl * 256), :]
        share = row_part[rows, :] / 4096.0
        for lane in range(0, B, 128):
            lanes = slice(lane, lane + 128)
            hat = tok[rows, lanes].astype(jnp.float32) * inv
            value = inv * (d_norm[rows, lanes] * gain[0:1, lanes] - hat * share)
            tokens_out[rows, lanes] = (gout[rows, lanes].astype(jnp.float32) + value).astype(jnp.bfloat16)

    loop(4, finish)
    gus[3].start_out(up_rows(3), local.at[4])
    b.wait()

    def mix(r):
        rows = chunk(r)
        mixed_out[rows, :] = (tok[rows, :].astype(jnp.float32) + b.result(rows)).astype(jnp.bfloat16)

    loop(4, mix)
    for copy in last_copies:
        copy.wait_recv()
    gain_out[...] = ((gain_terms[0] + gain_terms[1]) + (gain_terms[2] + gain_terms[3]))[0:1, :]
    for part in [gd] + gus:
        part.wait_out()
    wires.flush()


def block(tok, gout, gain, up, down, taps):
    vmem = pl.BlockSpec(memory_space=pltpu.VMEM)
    anywhere = pl.BlockSpec(memory_space=pl.ANY)
    bf16, f32 = jnp.bfloat16, jnp.float32
    blocks = lambda *shape: pltpu.VMEM(shape, bf16)
    floats = lambda *shape: pltpu.VMEM(shape, f32)
    return pl.pallas_call(
        block_kernel,
        out_shape=[
            jax.ShapeDtypeStruct((256, B), bf16),
            jax.ShapeDtypeStruct((256, B), bf16),
            jax.ShapeDtypeStruct((B, 2 * B), bf16),
            jax.ShapeDtypeStruct((2 * B, B), bf16),
            jax.ShapeDtypeStruct((32, 2 * B), f32),
            jax.ShapeDtypeStruct((1, B), f32),
        ],
        in_specs=[vmem, vmem, vmem, anywhere, anywhere, anywhere],
        out_specs=[vmem, vmem, anywhere, anywhere, vmem, vmem],
        scratch_shapes=[
            blocks(8, B, B),
            blocks(8, 2 * B, B),
            blocks(8, B, B),
            blocks(8, HID, B),
            blocks(8, B, B),
            blocks(8, 2 * B, B),
            floats(8, 8, B),
            floats(27, HID),
            floats(24, 10, 8, HID),
            floats(24, 10, 8, HID),
            floats(2 * B, HID),
            floats(2 * B, HID),
            blocks(2 * B, HID),
            blocks(B, B),
            floats(B, 128),
            blocks(2 * B, HID),
            blocks(B, HID),
            blocks(2, 2, 4, CHUNK, HID),
            blocks(2, 2, 4, CHUNK, HID),
            floats(256, B),
            floats(256, 128),
            floats(32, 8, HID),
            blocks(4, 32, HID),
            floats(2, 8, 256),
            floats(4, 8, 256),
            floats(4, 8, B),
            floats(4, 8, B),
        ]
        + RowScatter.scratch(2 * B, 3)
        + RowScatter.scratch(B, 1)
        + WeightScatter.scratch(HID)
        + WeightScatter.scratch(B)
        + [blocks(B, B)]
        + [pltpu.SemaphoreType.DMA((6,)), pltpu.SemaphoreType.DMA((200,)), pltpu.SemaphoreType.DMA((200,))],
        compiler_params=pltpu.CompilerParams(
            collective_id=0, has_side_effects=True, vmem_limit_bytes=62 << 20
        ),
        name="block",
    )(tok, gout, gain, up, down, taps)


def place_kernel(*refs):
    count = len(refs) // 3
    ins, outs, held, cut, sems = refs[:count], refs[count : 2 * count], refs[2 * count : -2], refs[-2], refs[-1]
    arriving = [pltpu.make_async_copy(src, mid, sems.at[0, i]) for i, (src, mid) in enumerate(zip(ins, held))]
    for copy in arriving:
        copy.start()
    leaving = []
    for i, (mid, dst) in enumerate(zip(held, outs)):
        arriving[i].wait()
        src = mid
        if mid.shape != dst.shape:
            cut[...] = mid[: dst.shape[0], :]
            src = cut
        leaving.append(pltpu.make_async_copy(src, dst, sems.at[1, i]))
        leaving[-1].start()
    for copy in leaving:
        copy.wait()


def place(arrays, rows):
    shapes = [(rows,) + a.shape[1:] if i == 4 else a.shape for i, a in enumerate(arrays)]
    specs = [pl.BlockSpec(memory_space=pl.ANY)] * len(arrays)
    return pl.pallas_call(
        place_kernel,
        out_shape=[jax.ShapeDtypeStruct(shape, a.dtype) for shape, a in zip(shapes, arrays)],
        in_specs=specs,
        out_specs=specs,
        scratch_shapes=[pltpu.VMEM(a.shape, a.dtype) for a in arrays]
        + [pltpu.VMEM(shapes[4], jnp.float32), pltpu.SemaphoreType.DMA((2, len(arrays)))],
        name="place",
    )(*arrays)


def per_device(tokens, grad_out, gain, up_weight, down_weight, conv_taps):
    tok = tokens.reshape(256, B)
    gout = grad_out.reshape(256, B)
    gain_rows = jnp.broadcast_to(gain[None], (8, B))
    outs = block(tok, gout, gain_rows, up_weight, down_weight, conv_taps)
    mixed, grad_tokens, grad_up, grad_down, grad_conv, grad_gain = place(outs, conv_taps.shape[0])
    return (
        mixed.reshape(tokens.shape),
        grad_tokens.reshape(tokens.shape),
        grad_up,
        grad_down,
        grad_conv,
        grad_gain.reshape(B),
    )


def solution(mesh):
    rows = P("dp", "seq", None, None, "fsdp")
    return jax.shard_map(
        per_device,
        mesh=mesh,
        in_specs=(rows, rows, P("fsdp"), P("seq", "fsdp"), P("fsdp", "seq"), P(None, "fsdp")),
        out_specs=(rows, rows, P("seq", "fsdp"), P("fsdp", "seq"), P(None, "fsdp"), P("fsdp")),
        check_vma=False,
    )
```

```python
import jax
import jax.numpy as jnp
from jax import lax
from jax.experimental import pallas as pl
from jax.experimental.pallas import tpu as pltpu
from jax.sharding import PartitionSpec as P

MESH = pl.DeviceIdType.MESH
gelu_scale = 0.7978845608028654
gelu_cubic = 0.044715
epsilon = 1e-06
B = 512


class Place:
    def __init__(self):
        self.zl = lax.axis_index("dp")
        self.f = lax.axis_index("fsdp")
        self.s = lax.axis_index("seq")
        self.x, self.c = lax.div(self.f, 2), lax.rem(self.f, 2)
        self.zh, self.y = lax.div(self.s, 4), lax.rem(self.s, 4)
        self.xs = [lax.rem(self.x + k, 4) for k in range(4)]
        self.ys = [lax.rem(self.y + k, 4) for k in range(4)]
        self.other_zl = {"dp": 1 - self.zl}
        self.other_core = {"fsdp": self.feat(0, 1)}
        self.x_up, self.x_down = {"fsdp": self.feat(1)}, {"fsdp": self.feat(3)}
        self.other_zh = {"seq": self.slab(0, 1)}
        self.y_up, self.y_down = {"seq": self.slab(1)}, {"seq": self.slab(3)}
        self.x_far, self.y_far = {"fsdp": self.feat(2)}, {"seq": self.slab(2)}
        self.diagonal = {"dp": 1 - self.zl, "seq": self.slab(0, 1)}
        self.rb = self.zl * 2 + self.zh
        self.z_peers = [
            (self.other_zl, (1 - self.zl) * 2 + self.zh),
            (self.other_zh, self.zl * 2 + 1 - self.zh),
            (self.diagonal, 3 - self.rb),
        ]
        self.x_peers = [self.x_up, self.x_far, self.x_down]
        self.y_peers = [self.y_up, self.y_far, self.y_down]

    def feat(self, k, flip=0):
        return self.xs[k] * 2 + (1 - self.c if flip else self.c)

    def slab(self, k, flip=0):
        return (1 - self.zh if flip else self.zh) * 4 + self.ys[k]

    def partners(self):
        return self.x_peers + self.y_peers + [where for where, _ in self.z_peers] + [self.other_core]


class Wires:
    def __init__(self, send, recv):
        self.send, self.recv, self.copies, self.left = send, recv, [], 0

    def start(self, src, dst, where):
        i = len(self.copies)
        copy = pltpu.make_async_remote_copy(
            src_ref=src, dst_ref=dst, send_sem=self.send.at[i], recv_sem=self.recv.at[i],
            device_id=where, device_id_type=MESH,
        )
        copy.start()
        self.copies.append(copy)
        return copy

    def flush(self, until=None):
        for copy in self.copies[self.left : until]:
            copy.wait_send()
        self.left = len(self.copies) if until is None else until


def meet(partners):
    barrier = pltpu.get_barrier_semaphore()
    for where in partners:
        pl.semaphore_signal(barrier, inc=1, device_id=where, device_id_type=MESH)
    pl.semaphore_wait(barrier, len(partners))


class WeightGather:
    def __init__(self, me, wires, own, for_other, buf):
        self.me, self.wires, self.own, self.for_other, self.buf = me, wires, own, for_other, buf
        self.half = buf.shape[1] // 2

    def start_z(self):
        self.z = self.wires.start(self.for_other, self.buf.at[self.me.s], self.me.other_zh)

    def start_y(self):
        self.up = self.wires.start(self.own, self.buf.at[self.me.s], self.me.y_up)
        self.down = self.wires.start(self.own, self.buf.at[self.me.s], self.me.y_down)

    def forward(self, flip):
        me, buf = self.me, self.buf
        below, above = me.slab(3, flip), me.slab(1, flip)
        self.up.wait_recv()
        part = buf.at[below, pl.ds(0, self.half)]
        first = self.wires.start(part, part, me.y_up)
        self.down.wait_recv()
        part = buf.at[above, pl.ds(self.half, self.half)]
        return first, self.wires.start(part, part, me.y_down)

    def forward_own(self):
        self.far = self.forward(0)

    def start_other(self):
        self.z.wait_recv()
        block = self.buf.at[self.me.slab(0, 1)]
        self.up = self.wires.start(block, block, self.me.y_up)
        self.down = self.wires.start(block, block, self.me.y_down)

    def forward_other(self):
        self.far_other = self.forward(1)

    def wait_far(self):
        for copy in self.far:
            copy.wait_recv()

    def wait_far_other(self):
        for copy in self.far_other:
            copy.wait_recv()


class TokenGather:
    def __init__(self, me, wires, own, buf, part, partners):
        self.me, self.wires, self.own, self.buf = me, wires, own, buf
        self.partners = [where for where, _ in partners]
        self.parts = [part] + [place for _, place in partners]
        self.ring, self.far, self.cores = {}, {}, []

    def rows(self, i, half=None):
        if half is None:
            return pl.ds(pl.multiple_of(self.parts[i] * 256, 256), 256)
        return pl.ds(pl.multiple_of(self.parts[i] * 256 + half * 128, 128), 128)

    def start_z(self):
        dst = self.buf.at[self.me.f, self.rows(0)]
        self.z = [self.wires.start(self.own, dst, where) for where in self.partners]

    def start(self, i):
        me = self.me
        dst = self.buf.at[me.f, self.rows(i)]
        src = dst if i else self.own
        if i:
            self.z[i - 1].wait_recv()
        self.ring[i] = [self.wires.start(src, dst, where) for where in (me.x_up, me.x_down)]
        self.cores.append(self.wires.start(src, dst, me.other_core))

    def to_core(self, k, i):
        block = self.buf.at[self.me.feat(k), self.rows(i)]
        self.cores.append(self.wires.start(block, block, self.me.other_core))

    def forward(self, i):
        me, buf = self.me, self.buf
        self.ring[i][0].wait_recv()
        part = buf.at[me.feat(3), self.rows(i, 0)]
        first = self.wires.start(part, part, me.x_up)
        self.ring[i][1].wait_recv()
        part = buf.at[me.feat(1), self.rows(i, 1)]
        self.far[i] = first, self.wires.start(part, part, me.x_down)
        self.to_core(3, i)
        self.to_core(1, i)

    def finish(self, i):
        for copy in self.far[i]:
            copy.wait_recv()
        self.to_core(2, i)

    def wait_cores(self):
        for copy in self.cores:
            copy.wait_recv()


CHUNK = 64
HID = 256


def chunk(r, base=0):
    return pl.ds(pl.multiple_of(base + r * CHUNK, CHUNK), CHUNK)


def loop(count, body):
    def step(i, carry):
        body(i)
        return carry

    lax.fori_loop(0, count, step, 0)


def add_into(dst, *parts):
    def body(r):
        rows = chunk(r)
        total = parts[0][rows, :].astype(jnp.float32)
        for part in parts[1:]:
            total = total + part[rows, :].astype(jnp.float32)
        dst[rows, :] = total.astype(dst.dtype)

    loop(dst.shape[0] // CHUNK, body)


class RowScatter:
    def __init__(self, me, wires, terms, part, partners, from_core, from_far, from_near, from_z):
        self.me, self.wires, self.terms = me, wires, terms
        self.part, self.partners = part, partners
        self.from_core, self.from_far, self.from_near = from_core, from_far, from_near
        self.from_z = from_z
        self.side = terms.shape[1] // 2

    def start_core(self):
        me = self.me
        self.core = {}
        for k in (2, 1, 3, 0):
            self.core[k] = self.wires.start(
                self.terms.at[me.feat(k, 1)], self.from_core.at[me.xs[k]], me.other_core
            )

    def held(self, k):
        return self.terms.at[self.me.feat(k)]

    def join(self, k):
        self.core[k].wait_recv()
        add_into(self.held(k), self.held(k), self.from_core.at[self.me.xs[k]])

    def start_far(self):
        me, side = self.me, self.side
        self.join(2)
        self.far = [
            self.wires.start(self.held(2).at[pl.ds(0, side)], self.from_far.at[0], me.x_up),
            self.wires.start(self.held(2).at[pl.ds(side, side)], self.from_far.at[1], me.x_down),
        ]
        self.join(1)
        self.join(3)
        self.near = [
            self.wires.start(self.held(1).at[pl.ds(side, side)], self.from_near.at[0, pl.ds(side, side)], me.x_up),
            self.wires.start(self.held(3).at[pl.ds(0, side)], self.from_near.at[1, pl.ds(0, side)], me.x_down),
        ]
        self.join(0)

    def start_near(self):
        me, side = self.me, self.side
        self.far[0].wait_recv()
        part = self.held(1).at[pl.ds(0, side)]
        add_into(part, part, self.from_far.at[0])
        self.near.append(self.wires.start(part, self.from_near.at[0, pl.ds(0, side)], me.x_up))
        self.far[1].wait_recv()
        part = self.held(3).at[pl.ds(side, side)]
        add_into(part, part, self.from_far.at[1])
        self.near.append(self.wires.start(part, self.from_near.at[1, pl.ds(side, side)], me.x_down))

    def sums(self, part):
        rows = pl.ds(pl.multiple_of(part * 256, 256), 256)
        return [self.held(0).at[rows], self.from_near.at[0, rows], self.from_near.at[1, rows]]

    def start_z(self):
        for copy in self.near:
            copy.wait_recv()
        self.z = []
        for i, (where, part) in enumerate(self.partners):
            sums = self.sums(part)
            add_into(sums[0], *sums)
            self.z.append(self.wires.start(sums[0], self.from_z.at[i], where))

    def wait(self):
        for copy in self.z:
            copy.wait_recv()
        self.all = self.sums(self.part) + [self.from_z.at[i] for i in range(len(self.z))]

    def result(self, rows):
        total = self.all[0][rows, :].astype(jnp.float32)
        for part in self.all[1:]:
            total = total + part[rows, :].astype(jnp.float32)
        return total

    @staticmethod
    def scratch(rows, partners):
        blocks = lambda *shape: pltpu.VMEM(shape, jnp.bfloat16)
        return [
            blocks(4, rows, B),
            blocks(2, rows // 2, B),
            blocks(2, rows, B),
            blocks(partners, 256, B),
        ]


class WeightScatter:
    def __init__(self, me, wires, terms, start, size, from_far, from_near):
        rows = pl.ds(start, size)
        self.me, self.wires, self.rows = me, wires, rows
        self.block = lambda j: terms.at[j, rows]
        self.from_far = [from_far.at[i, rows] for i in range(2)]
        self.from_near = lambda i: from_near.at[i, rows]

    def start_far(self):
        me, y = self.me, self.me.ys
        self.far = [
            self.wires.start(self.block(y[2]), self.from_far[0], me.y_up),
            self.wires.start(self.block(4 + y[2]), self.from_far[1], me.y_down),
        ]

    def start_direct(self):
        me, y = self.me, self.me.ys
        self.near = [
            self.wires.start(self.block(4 + y[1]), self.from_near(1), me.y_up),
            self.wires.start(self.block(y[3]), self.from_near(2), me.y_down),
        ]

    def start_near(self):
        me, y = self.me, self.me.ys
        self.far[0].wait_recv()
        block = self.block(y[1])
        add_into(block, block, self.from_far[0])
        self.near.append(self.wires.start(block, self.from_near(0), me.y_up))
        self.far[1].wait_recv()
        block = self.block(4 + y[3])
        add_into(block, block, self.from_far[1])
        self.near.append(self.wires.start(block, self.from_near(3), me.y_down))

    def parts(self, zh):
        return [self.block(zh * 4 + self.me.y), self.from_near(zh), self.from_near(2 + zh)]


    def start_z(self, from_z):
        for copy in self.near:
            copy.wait_recv()
        self.from_z = from_z.at[self.rows]
        other = self.block(self.me.slab(0, 1))
        add_into(other, *self.parts(1 - self.me.zh))
        self.z = self.wires.start(other, self.from_z, self.me.other_zh)

    def start_out(self, out, sem):
        self.z.wait_recv()
        block = self.block(self.me.s)
        add_into(block, *self.parts(self.me.zh), self.from_z)
        self.last = [self.wires.start(block, out, self.me.other_zl)]
        self.here = pltpu.make_async_copy(block, out, sem)
        self.here.start()


    def start_quarters(self, out, sem):
        me = self.me
        for copy in self.near:
            copy.wait_recv()
        mine, other = self.block(me.s), self.block(me.slab(0, 1))
        add_into(other, *self.parts(1 - me.zh))
        self.last = [self.wires.start(other, out, where) for where in (me.other_zh, me.diagonal)]
        add_into(mine, *self.parts(me.zh))
        self.last.append(self.wires.start(mine, out, me.other_zl))
        self.here = pltpu.make_async_copy(mine, out, sem)
        self.here.start()

    def wait_out(self):
        for copy in self.last:
            copy.wait_recv()
        self.here.wait()

    @staticmethod
    def scratch(rows):
        blocks = lambda *shape: pltpu.VMEM(shape, jnp.bfloat16)
        return [blocks(2, rows, B), blocks(4, rows, B)]


class Halo:
    def __init__(self, me, wires, planes, came, field):
        self.me, self.wires, self.planes, self.came, self.field = me, wires, planes, came, field

    def start(self):
        me = self.me
        self.copies = [
            self.wires.start(self.planes.at[1], self.came.at[0], me.y_up),
            self.wires.start(self.planes.at[0], self.came.at[1], me.y_down),
        ]

    def wait(self):
        for copy in self.copies:
            copy.wait_recv()
        low_inside = (self.me.y != 0).astype(jnp.float32)
        high_inside = (self.me.y != 3).astype(jnp.float32)
        for snap in range(2):
            low = [self.came[0, snap * 2 + zh].astype(jnp.float32) for zh in range(2)]
            high = [self.came[1, snap * 2 + zh].astype(jnp.float32) for zh in range(2)]
            edges = [
                (0, 0, low[0] * low_inside),
                (1, 0, low[1] * low_inside + low[0] * (1.0 - low_inside)),
                (0, 5, high[0] * high_inside + high[1] * (1.0 - high_inside)),
                (1, 5, high[1] * high_inside),
            ]
            for zh, place, plane in edges:
                self.field[(snap * 2 + zh) * 6 + place, 1:9] = plane.reshape(8, 8, HID)


def put_rows(part, rows_of, field, planes):
    for p in range(4):
        rounded = rows_of(p).astype(jnp.bfloat16)
        field[part * 6 + 1 + p, 1:9] = rounded.astype(jnp.float32).reshape(8, 8, HID)
        if p in (0, 3):
            planes[p // 3, part] = rounded


def shift(value, by):
    cells = lax.broadcasted_iota(jnp.int32, value.shape, 1)
    moved = pltpu.roll(value, by % 8, 1)
    return jnp.where(cells == (0 if by == 1 else 7), 0.0, moved)


def conv_planes(field, taps, flipped, count, which, finish):
    def body(i):
        part, p = which(i)
        for lane in range(0, HID, 128):
            lanes = pl.ds(lane, 128)
            by_c = [None] * 3
            for a in range(3):
                for b in range(3):
                    window = field[part * 6 + p + a, pl.ds(b, 8), :, lanes]
                    for c in range(3):
                        index = a * 9 + b * 3 + c
                        index = 26 - index if flipped else index
                        term = window * taps[pl.ds(index, 1), lanes].reshape(1, 1, 128)
                        by_c[c] = term if by_c[c] is None else by_c[c] + term
            total = by_c[1] + shift(by_c[0], 1) + shift(by_c[2], -1)
            finish(chunk(part * 4 + p), lanes, total.reshape(CHUNK, 128))

    loop(count, body)


def inner(i):
    return lax.div(i, 2), 1 + lax.rem(i, 2)


def outer(i):
    return lax.div(i, 2), 3 * lax.rem(i, 2)


def gelu_pair(preact):
    inner_value = gelu_scale * (preact + gelu_cubic * preact * preact * preact)
    tangent = jnp.tanh(inner_value)
    value = 0.5 * preact * (1.0 + tangent)
    slope = 0.5 * (1.0 + tangent) + 0.5 * preact * (1.0 - tangent * tangent) * gelu_scale * (
        1.0 + 3.0 * gelu_cubic * preact * preact
    )
    return (value, slope)


def dot(left, right, left_dim, right_dim):
    return lax.dot_general(
        left, right, (((left_dim,), (right_dim,)), ((), ())), preferred_element_type=jnp.float32
    )


def block_kernel(
    tok, gout, gain, up, down, taps_all,
    mixed_out, tokens_out, up_out, down_out, conv_out, gain_out,
    T, G, U, D, N, PB, gains, taps, field, d_field, total, slope, active, d_lifted, inverse,
    lift_here, lift_came, planes, came, d_norm, row_part, conv_sums, conv_terms, row_pair, row_terms,
    gain_z, gain_terms,
    b0, b1, b2, b3, n0, n1, n2, n3, w0, w1, v0, v1, v2,
    local, send, recv,
):
    me = Place()
    meet(me.partners())
    wires = Wires(send, recv)
    hidden = pl.ds(pl.multiple_of(me.zl * B, B), B)
    quarter = pl.ds(pl.multiple_of(me.rb * HID, HID), HID)
    other_quarter = pl.ds(pl.multiple_of((me.zl * 2 + 1 - me.zh) * HID, HID), HID)
    up_own, down_own = up.at[:, hidden], down.at[quarter, :]
    u = WeightGather(me, wires, up_own, up_own, U)
    d = WeightGather(me, wires, down_own, down.at[other_quarter, :], D)
    t = TokenGather(me, wires, tok, T, me.zl, [(me.other_zl, 1 - me.zl)])
    g = TokenGather(me, wires, gout, G, me.rb, me.z_peers)
    PN, GU, GD, d_slabs = N, G, T, lift_here
    b = RowScatter(me, wires, PB, me.rb, me.z_peers, b0, b1, b2, b3)
    n = RowScatter(me, wires, PN, me.zl, [(me.other_zl, 1 - me.zl)], n0, n1, n2, n3)
    gd = WeightScatter(me, wires, GD, 0, HID, w0, w1)
    gus = [WeightScatter(me, wires, GU, i * 128, 128, v0, v1) for i in range(4)]

    t.start_z()
    u.start_y()
    t.start(0)
    gain_copies = [wires.start(gain, gains.at[me.f], where) for where in me.x_peers + [me.other_core]]
    here = [
        pltpu.make_async_copy(src, dst, local.at[i])
        for i, (src, dst) in enumerate(
            [
                (tok, T.at[me.f, t.rows(0)]),
                (gain, gains.at[me.f]),
                (up_own, U.at[me.s]),
                (taps_all.at[:, quarter], taps),
                (gout, G.at[me.f, g.rows(0)]),
                (down_own, D.at[me.s]),
            ]
        )
    ]
    for copy in here:
        copy.start()
    u.start_z()
    g.start(0)
    field[...] = jnp.zeros_like(field)
    d_field[...] = jnp.zeros_like(d_field)
    t.forward(0)
    t.start(1)
    g.start_z()
    for copy in gain_copies[:3]:
        copy.wait_recv()
    for k in (1, 2, 3):
        block = gains.at[me.feat(k)]
        gain_copies.append(wires.start(block, block, me.other_core))
    u.forward_own()
    t.finish(0)
    g.forward(0)
    t.forward(1)
    u.start_other()
    d.start_z()
    g.start(1)
    t.finish(1)
    d.start_y()
    g.start(2)
    for copy in here:
        copy.wait()
    for copy in gain_copies[3:]:
        copy.wait_recv()
    t.wait_cores()

    def normalise(r):
        rows = chunk(r)
        squares = jnp.zeros((CHUNK, 128), jnp.float32)
        for k in range(8):
            for lane in range(0, B, 128):
                value = T[k, rows, pl.ds(lane, 128)].astype(jnp.float32)
                squares = squares + value * value
        mean = jnp.sum(squares, axis=1, keepdims=True) / 4096.0
        inv = jnp.broadcast_to(lax.rsqrt(mean + epsilon), (CHUNK, 128))
        inverse[rows, :] = inv
        for k in range(8):
            for lane in range(0, B, 128):
                lanes = pl.ds(lane, 128)
                value = T[k, rows, lanes].astype(jnp.float32) * inv * gains[k, 0:1, lanes]
                N[k, rows, lanes] = value.astype(jnp.bfloat16)

    loop(8, normalise)
    total[...] = jnp.zeros_like(total)

    def lift(zh):
        def body(i):
            j = zh * 4 + i
            for half in range(2):
                total[pl.ds(half * B, B), :] += dot(N[j], U[j, :, pl.ds(half * HID, HID)], 1, 0)

        loop(4, body)

    u.wait_far()
    g.finish(0)
    g.forward(1)
    lift(me.zh)
    u.forward_other()
    d.forward_own()
    g.start(3)
    d.start_other()
    g.finish(1)
    g.forward(2)
    u.wait_far_other()
    lift(1 - me.zh)

    def round_lift(r):
        lift_here[chunk(r), :] = total[chunk(r), :].astype(jnp.bfloat16)

    loop(16, round_lift)
    lift_side = lambda zh: lift_here.at[pl.ds(pl.multiple_of(zh * B, B), B)]
    lift_copy = wires.start(lift_side(1 - me.zh), lift_came, me.other_zh)
    g.forward(3)
    d.wait_far()
    d.forward_other()
    g.finish(2)
    mine = lift_side(me.zh)
    for snap in range(2):
        put_rows(snap * 2 + me.zh, lambda p: mine[pl.ds(snap * 256 + p * CHUNK, CHUNK), :], field, planes.at[0])
    lift_copy.wait_recv()
    for snap in range(2):
        put_rows(
            snap * 2 + 1 - me.zh, lambda p: lift_came[pl.ds(snap * 256 + p * CHUNK, CHUNK), :], field, planes.at[0]
        )
    halo = Halo(me, wires, planes.at[0], came.at[0], field)
    halo.start()

    def activate(rows, lanes, preact):
        value, rate = gelu_pair(preact)
        active[rows, lanes] = value.astype(jnp.bfloat16)
        slope[rows, lanes] = rate

    conv_planes(field, taps, False, 8, inner, activate)
    halo.wait()
    conv_planes(field, taps, False, 8, outer, activate)
    d.wait_far_other()

    def branch_term(j):
        PB[j] = dot(active[...], D[j], 1, 0).astype(jnp.bfloat16)

    loop(8, branch_term)
    b.start_core()
    g.finish(3)
    g.wait_cores()
    gathered = len(wires.copies)
    total[...] = jnp.zeros_like(total)

    def d_active(j):
        total[...] += dot(G[j], D[j], 1, 1)

    loop(8, d_active)

    def d_preact(i):
        part = i
        put_rows(
            part,
            lambda p: total[chunk(part * 4 + p), :] * slope[chunk(part * 4 + p), :],
            d_field,
            planes.at[1],
        )

    loop(4, d_preact)
    d_halo = Halo(me, wires, planes.at[1], came.at[1], d_field)
    d_halo.start()

    b.start_far()
    wires.flush(gathered)

    def down_term(j):
        GD[j, pl.ds(0, HID), :] = dot(active[...], G[j], 0, 0).astype(jnp.bfloat16)

    loop(8, down_term)
    gd.start_far()
    gd.start_direct()

    def d_lift(rows, lanes, value):
        d_slabs[rows, lanes] = value.astype(jnp.bfloat16)

    conv_planes(d_field, taps, True, 8, inner, d_lift)
    d_halo.wait()
    conv_planes(d_field, taps, True, 8, outer, d_lift)
    d_columns = pl.ds(pl.multiple_of(me.zh * HID, HID), HID)
    d_copies = [
        wires.start(
            d_slabs.at[pl.ds(pl.multiple_of((snap * 2 + 1 - me.zh) * 256, 256), 256), :],
            d_lifted.at[pl.ds(snap * 256, 256), d_columns],
            me.other_zh,
        )
        for snap in range(2)
    ]
    gd.start_near()
    for snap in range(2):
        d_lifted[pl.ds(snap * 256, 256), d_columns] = d_slabs[
            pl.ds(pl.multiple_of((snap * 2 + me.zh) * 256, 256), 256), :
        ]
    for copy in d_copies:
        copy.wait_recv()
    b.start_near()

    def up_term(j):
        GU[j, pl.ds(0, B), :] = dot(N[j], d_lifted[...], 0, 0).astype(jnp.bfloat16)

    loop(8, up_term)
    for part in gus:
        part.start_far()
    gd.start_quarters(down_out.at[quarter, :], local.at[0])

    def norm_term(j):
        PN[j] = dot(d_lifted[...], U[j], 1, 1).astype(jnp.bfloat16)

    loop(8, norm_term)
    n.start_core()
    n.start_far()

    conv_sums[...] = jnp.zeros_like(conv_sums)

    def taps_grad(i):
        part, p = lax.div(i, 4), lax.rem(i, 4)
        for lane in range(0, HID, 128):
            lanes = pl.ds(lane, 128)
            here_d = d_field[part * 6 + 1 + p, pl.ds(1, 8), :, lanes]
            by_c = [shift(here_d, -1), here_d, shift(here_d, 1)]
            for a in range(3):
                for b_ in range(3):
                    window = field[part * 6 + p + a, pl.ds(b_, 8), :, lanes]
                    for c in range(3):
                        term = jnp.sum(by_c[c] * window, axis=0)
                        conv_sums[a * 9 + b_ * 3 + c, :, lanes] += term

    loop(16, taps_grad)
    conv_terms[me.y] = jnp.sum(conv_sums[...], axis=1).astype(jnp.bfloat16)
    conv_copies = [wires.start(conv_terms.at[me.y], conv_terms.at[me.y], where) for where in me.y_peers]

    b.start_z()
    for part in gus[:2]:
        part.start_direct()
        part.start_near()
    n.start_near()
    for copy in conv_copies:
        copy.wait_recv()
    conv = conv_terms[0].astype(jnp.float32)
    for k in range(1, 4):
        conv = conv + conv_terms[k].astype(jnp.float32)
    conv_here = conv_out.at[:, quarter]
    conv_here[...] = conv
    last_copies = [wires.start(conv_here, conv_here, where) for where, _ in me.z_peers]
    gus[0].start_z(v2)
    gus[2].start_direct()
    gus[2].start_near()
    n.start_z()
    gus[1].start_z(v2)
    gus[3].start_direct()
    gus[3].start_near()
    up_rows = lambda i: up_out.at[pl.ds(i * 128, 128), hidden]
    gus[0].start_out(up_rows(0), local.at[1])
    gus[2].start_z(v2)
    n.wait()

    def rows_part(r, gain_sum):
        rows = chunk(r)
        whole = n.result(rows)
        d_norm[rows, :] = whole
        inv = inverse[chunk(r, me.zl * 256), :]
        part = jnp.zeros((CHUNK, 128), jnp.float32)
        sums = []
        for lane in range(0, B, 128):
            lanes = slice(lane, lane + 128)
            with_hat = whole[:, lanes] * (tok[rows, lanes].astype(jnp.float32) * inv)
            part = part + with_hat * gain[0:1, lanes]
            sums.append(jnp.sum(with_hat.reshape(8, 8, 128), axis=0))
        row_part[rows, :] = part
        return gain_sum + jnp.concatenate(sums, axis=1)

    gain_sum = lax.fori_loop(0, 4, rows_part, jnp.zeros((8, B), jnp.float32))
    row_sum = jnp.sum(jnp.transpose(row_part[...]), axis=0, keepdims=True)
    row_pair[me.c] = jnp.broadcast_to(row_sum, (8, 256))
    row_copy = wires.start(row_pair.at[me.c], row_pair.at[me.c], me.other_core)
    gain_z[me.rb] = jnp.broadcast_to(jnp.sum(gain_sum, axis=0, keepdims=True), (8, B))
    gain_copies = [wires.start(gain_z.at[me.rb], gain_z.at[me.rb], where) for where, _ in me.z_peers]
    row_copy.wait_recv()
    row_terms[me.x] = row_pair[0] + row_pair[1]
    row_copies = [wires.start(row_terms.at[me.x], row_terms.at[me.x], where) for where in me.x_peers]
    gus[3].start_z(v2)
    gus[1].start_out(up_rows(1), local.at[2])
    gus[2].start_out(up_rows(2), local.at[3])
    for copy in gain_copies:
        copy.wait_recv()
    gain_terms[me.y] = (gain_z[0] + gain_z[1]) + (gain_z[2] + gain_z[3])
    last_copies += [wires.start(gain_terms.at[me.y], gain_terms.at[me.y], where) for where in me.y_peers]
    for copy in row_copies:
        copy.wait_recv()
    rows_sum = (row_terms[0] + row_terms[1]) + (row_terms[2] + row_terms[3])
    row_part[...] = jnp.transpose(jnp.broadcast_to(rows_sum[0:1, :], (128, 256)))
    gus[3].start_out(up_rows(3), local.at[4])

    def finish(r):
        rows = chunk(r)
        inv = inverse[chunk(r, me.zl * 256), :]
        share = row_part[rows, :] / 4096.0
        for lane in range(0, B, 128):
            lanes = slice(lane, lane + 128)
            hat = tok[rows, lanes].astype(jnp.float32) * inv
            value = inv * (d_norm[rows, lanes] * gain[0:1, lanes] - hat * share)
            tokens_out[rows, lanes] = (gout[rows, lanes].astype(jnp.float32) + value).astype(jnp.bfloat16)

    loop(4, finish)
    b.wait()

    def mix(r):
        rows = chunk(r)
        mixed_out[rows, :] = (tok[rows, :].astype(jnp.float32) + b.result(rows)).astype(jnp.bfloat16)

    loop(4, mix)
    for copy in last_copies:
        copy.wait_recv()
    gain_out[...] = ((gain_terms[0] + gain_terms[1]) + (gain_terms[2] + gain_terms[3]))[0:1, :]
    for part in [gd] + gus:
        part.wait_out()
    wires.flush()


def block(tok, gout, gain, up, down, taps):
    vmem = pl.BlockSpec(memory_space=pltpu.VMEM)
    anywhere = pl.BlockSpec(memory_space=pl.ANY)
    bf16, f32 = jnp.bfloat16, jnp.float32
    blocks = lambda *shape: pltpu.VMEM(shape, bf16)
    floats = lambda *shape: pltpu.VMEM(shape, f32)
    return pl.pallas_call(
        block_kernel,
        out_shape=[
            jax.ShapeDtypeStruct((256, B), bf16),
            jax.ShapeDtypeStruct((256, B), bf16),
            jax.ShapeDtypeStruct((B, 2 * B), bf16),
            jax.ShapeDtypeStruct((2 * B, B), bf16),
            jax.ShapeDtypeStruct((32, 2 * B), f32),
            jax.ShapeDtypeStruct((1, B), f32),
        ],
        in_specs=[vmem, vmem, vmem, anywhere, anywhere, anywhere],
        out_specs=[vmem, vmem, anywhere, anywhere, vmem, vmem],
        scratch_shapes=[
            blocks(8, B, B),
            blocks(8, 2 * B, B),
            blocks(8, B, B),
            blocks(8, HID, B),
            blocks(8, B, B),
            blocks(8, 2 * B, B),
            floats(8, 8, B),
            floats(27, HID),
            floats(24, 10, 8, HID),
            floats(24, 10, 8, HID),
            floats(2 * B, HID),
            floats(2 * B, HID),
            blocks(2 * B, HID),
            blocks(B, B),
            floats(B, 128),
            blocks(2 * B, HID),
            blocks(B, HID),
            blocks(2, 2, 4, CHUNK, HID),
            blocks(2, 2, 4, CHUNK, HID),
            floats(256, B),
            floats(256, 128),
            floats(32, 8, HID),
            blocks(4, 32, HID),
            floats(2, 8, 256),
            floats(4, 8, 256),
            floats(4, 8, B),
            floats(4, 8, B),
        ]
        + RowScatter.scratch(2 * B, 3)
        + RowScatter.scratch(B, 1)
        + WeightScatter.scratch(HID)
        + WeightScatter.scratch(B)
        + [blocks(B, B)]
        + [pltpu.SemaphoreType.DMA((6,)), pltpu.SemaphoreType.DMA((200,)), pltpu.SemaphoreType.DMA((200,))],
        compiler_params=pltpu.CompilerParams(
            collective_id=0, has_side_effects=True, vmem_limit_bytes=62 << 20
        ),
        name="block",
    )(tok, gout, gain, up, down, taps)


def place_kernel(*refs):
    count = len(refs) // 3
    ins, outs, held, cut, sems = refs[:count], refs[count : 2 * count], refs[2 * count : -2], refs[-2], refs[-1]
    arriving = [pltpu.make_async_copy(src, mid, sems.at[0, i]) for i, (src, mid) in enumerate(zip(ins, held))]
    for copy in arriving:
        copy.start()
    leaving = []
    for i, (mid, dst) in enumerate(zip(held, outs)):
        arriving[i].wait()
        src = mid
        if mid.shape != dst.shape:
            cut[...] = mid[: dst.shape[0], :]
            src = cut
        leaving.append(pltpu.make_async_copy(src, dst, sems.at[1, i]))
        leaving[-1].start()
    for copy in leaving:
        copy.wait()


def place(arrays, rows):
    shapes = [(rows,) + a.shape[1:] if i == 4 else a.shape for i, a in enumerate(arrays)]
    specs = [pl.BlockSpec(memory_space=pl.ANY)] * len(arrays)
    return pl.pallas_call(
        place_kernel,
        out_shape=[jax.ShapeDtypeStruct(shape, a.dtype) for shape, a in zip(shapes, arrays)],
        in_specs=specs,
        out_specs=specs,
        scratch_shapes=[pltpu.VMEM(a.shape, a.dtype) for a in arrays]
        + [pltpu.VMEM(shapes[4], jnp.float32), pltpu.SemaphoreType.DMA((2, len(arrays)))],
        name="place",
    )(*arrays)


def per_device(tokens, grad_out, gain, up_weight, down_weight, conv_taps):
    tok = tokens.reshape(256, B)
    gout = grad_out.reshape(256, B)
    gain_rows = jnp.broadcast_to(gain[None], (8, B))
    outs = block(tok, gout, gain_rows, up_weight, down_weight, conv_taps)
    mixed, grad_tokens, grad_up, grad_down, grad_conv, grad_gain = place(outs, conv_taps.shape[0])
    return (
        mixed.reshape(tokens.shape),
        grad_tokens.reshape(tokens.shape),
        grad_up,
        grad_down,
        grad_conv,
        grad_gain.reshape(B),
    )


def solution(mesh):
    rows = P("dp", "seq", None, None, "fsdp")
    return jax.shard_map(
        per_device,
        mesh=mesh,
        in_specs=(rows, rows, P("fsdp"), P("seq", "fsdp"), P("fsdp", "seq"), P(None, "fsdp")),
        out_specs=(rows, rows, P("seq", "fsdp"), P("fsdp", "seq"), P(None, "fsdp"), P("fsdp")),
        check_vma=False,
    )
```

```python
import jax
import jax.numpy as jnp
from jax import lax
from jax.experimental import pallas as pl
from jax.experimental.pallas import tpu as pltpu
from jax.sharding import PartitionSpec as P

MESH = pl.DeviceIdType.MESH
gelu_scale = 0.7978845608028654
gelu_cubic = 0.044715
epsilon = 1e-06
B = 512


class Place:
    def __init__(self):
        self.zl = lax.axis_index("dp")
        self.f = lax.axis_index("fsdp")
        self.s = lax.axis_index("seq")
        self.x, self.c = lax.div(self.f, 2), lax.rem(self.f, 2)
        self.zh, self.y = lax.div(self.s, 4), lax.rem(self.s, 4)
        self.xs = [lax.rem(self.x + k, 4) for k in range(4)]
        self.ys = [lax.rem(self.y + k, 4) for k in range(4)]
        self.other_zl = {"dp": 1 - self.zl}
        self.other_core = {"fsdp": self.feat(0, 1)}
        self.x_up, self.x_down = {"fsdp": self.feat(1)}, {"fsdp": self.feat(3)}
        self.other_zh = {"seq": self.slab(0, 1)}
        self.y_up, self.y_down = {"seq": self.slab(1)}, {"seq": self.slab(3)}
        self.x_far, self.y_far = {"fsdp": self.feat(2)}, {"seq": self.slab(2)}
        self.diagonal = {"dp": 1 - self.zl, "seq": self.slab(0, 1)}
        self.rb = self.zl * 2 + self.zh
        self.z_peers = [
            (self.other_zl, (1 - self.zl) * 2 + self.zh),
            (self.other_zh, self.zl * 2 + 1 - self.zh),
            (self.diagonal, 3 - self.rb),
        ]
        self.x_peers = [self.x_up, self.x_far, self.x_down]
        self.y_peers = [self.y_up, self.y_far, self.y_down]

    def feat(self, k, flip=0):
        return self.xs[k] * 2 + (1 - self.c if flip else self.c)

    def slab(self, k, flip=0):
        return (1 - self.zh if flip else self.zh) * 4 + self.ys[k]

    def partners(self):
        return self.x_peers + self.y_peers + [where for where, _ in self.z_peers] + [self.other_core]


class Wires:
    def __init__(self, send, recv):
        self.send, self.recv, self.copies, self.left = send, recv, [], 0

    def start(self, src, dst, where):
        i = len(self.copies)
        copy = pltpu.make_async_remote_copy(
            src_ref=src, dst_ref=dst, send_sem=self.send.at[i], recv_sem=self.recv.at[i],
            device_id=where, device_id_type=MESH,
        )
        copy.start()
        self.copies.append(copy)
        return copy

    def flush(self, until=None):
        for copy in self.copies[self.left : until]:
            copy.wait_send()
        self.left = len(self.copies) if until is None else until


def meet(partners):
    barrier = pltpu.get_barrier_semaphore()
    for where in partners:
        pl.semaphore_signal(barrier, inc=1, device_id=where, device_id_type=MESH)
    pl.semaphore_wait(barrier, len(partners))


class WeightGather:
    def __init__(self, me, wires, own, for_other, buf):
        self.me, self.wires, self.own, self.for_other, self.buf = me, wires, own, for_other, buf
        self.half = buf.shape[1] // 2

    def start_z(self):
        self.z = self.wires.start(self.for_other, self.buf.at[self.me.s], self.me.other_zh)

    def start_y(self):
        self.up = self.wires.start(self.own, self.buf.at[self.me.s], self.me.y_up)
        self.down = self.wires.start(self.own, self.buf.at[self.me.s], self.me.y_down)

    def forward(self, flip):
        me, buf = self.me, self.buf
        below, above = me.slab(3, flip), me.slab(1, flip)
        self.up.wait_recv()
        part = buf.at[below, pl.ds(0, self.half)]
        first = self.wires.start(part, part, me.y_up)
        self.down.wait_recv()
        part = buf.at[above, pl.ds(self.half, self.half)]
        return first, self.wires.start(part, part, me.y_down)

    def forward_own(self):
        self.far = self.forward(0)

    def start_other(self):
        self.z.wait_recv()
        block = self.buf.at[self.me.slab(0, 1)]
        self.up = self.wires.start(block, block, self.me.y_up)
        self.down = self.wires.start(block, block, self.me.y_down)

    def forward_other(self):
        self.far_other = self.forward(1)

    def wait_far(self):
        for copy in self.far:
            copy.wait_recv()

    def wait_far_other(self):
        for copy in self.far_other:
            copy.wait_recv()


class TokenGather:
    def __init__(self, me, wires, own, buf, part, partners):
        self.me, self.wires, self.own, self.buf = me, wires, own, buf
        self.partners = [where for where, _ in partners]
        self.parts = [part] + [place for _, place in partners]
        self.ring, self.far, self.cores = {}, {}, []

    def rows(self, i, half=None):
        if half is None:
            return pl.ds(pl.multiple_of(self.parts[i] * 256, 256), 256)
        return pl.ds(pl.multiple_of(self.parts[i] * 256 + half * 128, 128), 128)

    def start_z(self):
        dst = self.buf.at[self.me.f, self.rows(0)]
        self.z = [self.wires.start(self.own, dst, where) for where in self.partners]

    def start(self, i):
        me = self.me
        dst = self.buf.at[me.f, self.rows(i)]
        src = dst if i else self.own
        if i:
            self.z[i - 1].wait_recv()
        self.ring[i] = [self.wires.start(src, dst, where) for where in (me.x_up, me.x_down)]
        self.cores.append(self.wires.start(src, dst, me.other_core))

    def to_core(self, k, i):
        block = self.buf.at[self.me.feat(k), self.rows(i)]
        self.cores.append(self.wires.start(block, block, self.me.other_core))

    def forward(self, i):
        me, buf = self.me, self.buf
        self.ring[i][0].wait_recv()
        part = buf.at[me.feat(3), self.rows(i, 0)]
        first = self.wires.start(part, part, me.x_up)
        self.ring[i][1].wait_recv()
        part = buf.at[me.feat(1), self.rows(i, 1)]
        self.far[i] = first, self.wires.start(part, part, me.x_down)
        self.to_core(3, i)
        self.to_core(1, i)

    def finish(self, i):
        for copy in self.far[i]:
            copy.wait_recv()
        self.to_core(2, i)

    def wait_cores(self):
        for copy in self.cores:
            copy.wait_recv()


CHUNK = 64
HID = 256


def chunk(r, base=0):
    return pl.ds(pl.multiple_of(base + r * CHUNK, CHUNK), CHUNK)


def loop(count, body):
    def step(i, carry):
        body(i)
        return carry

    lax.fori_loop(0, count, step, 0)


def add_into(dst, *parts):
    def body(r):
        rows = chunk(r)
        total = parts[0][rows, :].astype(jnp.float32)
        for part in parts[1:]:
            total = total + part[rows, :].astype(jnp.float32)
        dst[rows, :] = total.astype(dst.dtype)

    loop(dst.shape[0] // CHUNK, body)


class RowScatter:
    def __init__(self, me, wires, terms, part, partners, from_core, from_far, from_near, from_z):
        self.me, self.wires, self.terms = me, wires, terms
        self.part, self.partners = part, partners
        self.from_core, self.from_far, self.from_near = from_core, from_far, from_near
        self.from_z = from_z
        self.side = terms.shape[1] // 2

    def start_core(self):
        me = self.me
        self.core = {}
        for k in (2, 1, 3, 0):
            self.core[k] = self.wires.start(
                self.terms.at[me.feat(k, 1)], self.from_core.at[me.xs[k]], me.other_core
            )

    def held(self, k):
        return self.terms.at[self.me.feat(k)]

    def join(self, k):
        self.core[k].wait_recv()
        add_into(self.held(k), self.held(k), self.from_core.at[self.me.xs[k]])

    def start_far(self):
        me, side = self.me, self.side
        self.join(2)
        self.far = [
            self.wires.start(self.held(2).at[pl.ds(0, side)], self.from_far.at[0], me.x_up),
            self.wires.start(self.held(2).at[pl.ds(side, side)], self.from_far.at[1], me.x_down),
        ]
        self.join(1)
        self.join(3)
        self.near = [
            self.wires.start(self.held(1).at[pl.ds(side, side)], self.from_near.at[0, pl.ds(side, side)], me.x_up),
            self.wires.start(self.held(3).at[pl.ds(0, side)], self.from_near.at[1, pl.ds(0, side)], me.x_down),
        ]
        self.join(0)

    def start_near(self):
        me, side = self.me, self.side
        self.far[0].wait_recv()
        part = self.held(1).at[pl.ds(0, side)]
        add_into(part, part, self.from_far.at[0])
        self.near.append(self.wires.start(part, self.from_near.at[0, pl.ds(0, side)], me.x_up))
        self.far[1].wait_recv()
        part = self.held(3).at[pl.ds(side, side)]
        add_into(part, part, self.from_far.at[1])
        self.near.append(self.wires.start(part, self.from_near.at[1, pl.ds(side, side)], me.x_down))

    def sums(self, part):
        rows = pl.ds(pl.multiple_of(part * 256, 256), 256)
        return [self.held(0).at[rows], self.from_near.at[0, rows], self.from_near.at[1, rows]]

    def start_z(self):
        for copy in self.near:
            copy.wait_recv()
        self.z = []
        for i, (where, part) in enumerate(self.partners):
            sums = self.sums(part)
            add_into(sums[0], *sums)
            self.z.append(self.wires.start(sums[0], self.from_z.at[i], where))

    def wait(self):
        for copy in self.z:
            copy.wait_recv()
        self.all = self.sums(self.part) + [self.from_z.at[i] for i in range(len(self.z))]

    def result(self, rows):
        total = self.all[0][rows, :].astype(jnp.float32)
        for part in self.all[1:]:
            total = total + part[rows, :].astype(jnp.float32)
        return total

    @staticmethod
    def scratch(rows, partners):
        blocks = lambda *shape: pltpu.VMEM(shape, jnp.bfloat16)
        return [
            blocks(4, rows, B),
            blocks(2, rows // 2, B),
            blocks(2, rows, B),
            blocks(partners, 256, B),
        ]


class WeightScatter:
    def __init__(self, me, wires, terms, start, size, from_far, from_near):
        rows = pl.ds(start, size)
        self.me, self.wires, self.rows = me, wires, rows
        self.block = lambda j: terms.at[j, rows]
        self.from_far = [from_far.at[i, rows] for i in range(2)]
        self.from_near = lambda i: from_near.at[i, rows]

    def start_far(self):
        me, y = self.me, self.me.ys
        self.far = [
            self.wires.start(self.block(y[2]), self.from_far[0], me.y_up),
            self.wires.start(self.block(4 + y[2]), self.from_far[1], me.y_down),
        ]

    def start_direct(self):
        me, y = self.me, self.me.ys
        self.near = [
            self.wires.start(self.block(4 + y[1]), self.from_near(1), me.y_up),
            self.wires.start(self.block(y[3]), self.from_near(2), me.y_down),
        ]

    def start_near(self):
        me, y = self.me, self.me.ys
        self.far[0].wait_recv()
        block = self.block(y[1])
        add_into(block, block, self.from_far[0])
        self.near.append(self.wires.start(block, self.from_near(0), me.y_up))
        self.far[1].wait_recv()
        block = self.block(4 + y[3])
        add_into(block, block, self.from_far[1])
        self.near.append(self.wires.start(block, self.from_near(3), me.y_down))

    def parts(self, zh):
        return [self.block(zh * 4 + self.me.y), self.from_near(zh), self.from_near(2 + zh)]


    def start_z(self, from_z):
        for copy in self.near:
            copy.wait_recv()
        self.from_z = from_z.at[self.rows]
        other = self.block(self.me.slab(0, 1))
        add_into(other, *self.parts(1 - self.me.zh))
        self.z = self.wires.start(other, self.from_z, self.me.other_zh)

    def start_out(self, out, sem):
        self.z.wait_recv()
        block = self.block(self.me.s)
        add_into(block, *self.parts(self.me.zh), self.from_z)
        self.last = [self.wires.start(block, out, self.me.other_zl)]
        self.here = pltpu.make_async_copy(block, out, sem)
        self.here.start()


    def start_quarters(self, out, sem):
        me = self.me
        for copy in self.near:
            copy.wait_recv()
        mine, other = self.block(me.s), self.block(me.slab(0, 1))
        add_into(other, *self.parts(1 - me.zh))
        self.last = [self.wires.start(other, out, where) for where in (me.other_zh, me.diagonal)]
        add_into(mine, *self.parts(me.zh))
        self.last.append(self.wires.start(mine, out, me.other_zl))
        self.here = pltpu.make_async_copy(mine, out, sem)
        self.here.start()

    def wait_out(self):
        for copy in self.last:
            copy.wait_recv()
        self.here.wait()

    @staticmethod
    def scratch(rows):
        blocks = lambda *shape: pltpu.VMEM(shape, jnp.bfloat16)
        return [blocks(2, rows, B), blocks(4, rows, B)]


class Halo:
    def __init__(self, me, wires, planes, came, field):
        self.me, self.wires, self.planes, self.came, self.field = me, wires, planes, came, field

    def start(self):
        me = self.me
        self.copies = [
            self.wires.start(self.planes.at[1], self.came.at[0], me.y_up),
            self.wires.start(self.planes.at[0], self.came.at[1], me.y_down),
        ]

    def wait(self):
        for copy in self.copies:
            copy.wait_recv()
        low_inside = (self.me.y != 0).astype(jnp.float32)
        high_inside = (self.me.y != 3).astype(jnp.float32)
        for snap in range(2):
            low = [self.came[0, snap * 2 + zh].astype(jnp.float32) for zh in range(2)]
            high = [self.came[1, snap * 2 + zh].astype(jnp.float32) for zh in range(2)]
            edges = [
                (0, 0, low[0] * low_inside),
                (1, 0, low[1] * low_inside + low[0] * (1.0 - low_inside)),
                (0, 5, high[0] * high_inside + high[1] * (1.0 - high_inside)),
                (1, 5, high[1] * high_inside),
            ]
            for zh, place, plane in edges:
                self.field[(snap * 2 + zh) * 6 + place, 1:9] = plane.reshape(8, 8, HID)


def put_rows(part, rows_of, field, planes):
    for p in range(4):
        rounded = rows_of(p).astype(jnp.bfloat16)
        field[part * 6 + 1 + p, 1:9] = rounded.astype(jnp.float32).reshape(8, 8, HID)
        if p in (0, 3):
            planes[p // 3, part] = rounded


def shift(value, by):
    cells = lax.broadcasted_iota(jnp.int32, value.shape, 1)
    moved = pltpu.roll(value, by % 8, 1)
    return jnp.where(cells == (0 if by == 1 else 7), 0.0, moved)


def conv_planes(field, taps, flipped, count, which, finish):
    def body(i):
        part, p = which(i)
        for lane in range(0, HID, 128):
            lanes = pl.ds(lane, 128)
            by_c = [None] * 3
            for a in range(3):
                for b in range(3):
                    window = field[part * 6 + p + a, pl.ds(b, 8), :, lanes]
                    for c in range(3):
                        index = a * 9 + b * 3 + c
                        index = 26 - index if flipped else index
                        term = window * taps[pl.ds(index, 1), lanes].reshape(1, 1, 128)
                        by_c[c] = term if by_c[c] is None else by_c[c] + term
            total = by_c[1] + shift(by_c[0], 1) + shift(by_c[2], -1)
            finish(chunk(part * 4 + p), lanes, total.reshape(CHUNK, 128))

    loop(count, body)


def inner(i):
    return lax.div(i, 2), 1 + lax.rem(i, 2)


def outer(i):
    return lax.div(i, 2), 3 * lax.rem(i, 2)


def gelu_pair(preact):
    inner_value = gelu_scale * (preact + gelu_cubic * preact * preact * preact)
    tangent = jnp.tanh(inner_value)
    value = 0.5 * preact * (1.0 + tangent)
    slope = 0.5 * (1.0 + tangent) + 0.5 * preact * (1.0 - tangent * tangent) * gelu_scale * (
        1.0 + 3.0 * gelu_cubic * preact * preact
    )
    return (value, slope)


def dot(left, right, left_dim, right_dim):
    return lax.dot_general(
        left, right, (((left_dim,), (right_dim,)), ((), ())), preferred_element_type=jnp.float32
    )


def block_kernel(
    tok, gout, gain, up, down, taps_all,
    mixed_out, tokens_out, up_out, down_out, conv_out, gain_out,
    T, G, U, D, N, PB, gains, taps, field, d_field, total, slope, active, d_lifted, inverse,
    lift_here, lift_came, planes, came, d_norm, row_part, conv_sums, conv_terms, row_pair, row_terms,
    gain_z, gain_terms,
    b0, b1, b2, b3, n0, n1, n2, n3, w0, w1, v0, v1, v2,
    local, send, recv,
):
    me = Place()
    meet(me.partners())
    wires = Wires(send, recv)
    hidden = pl.ds(pl.multiple_of(me.zl * B, B), B)
    quarter = pl.ds(pl.multiple_of(me.rb * HID, HID), HID)
    other_quarter = pl.ds(pl.multiple_of((me.zl * 2 + 1 - me.zh) * HID, HID), HID)
    up_own, down_own = up.at[:, hidden], down.at[quarter, :]
    u = WeightGather(me, wires, up_own, up_own, U)
    d = WeightGather(me, wires, down_own, down.at[other_quarter, :], D)
    t = TokenGather(me, wires, tok, T, me.zl, [(me.other_zl, 1 - me.zl)])
    g = TokenGather(me, wires, gout, G, me.rb, me.z_peers)
    PN, GU, GD, d_slabs = N, G, T, lift_here
    b = RowScatter(me, wires, PB, me.rb, me.z_peers, b0, b1, b2, b3)
    n = RowScatter(me, wires, PN, me.zl, [(me.other_zl, 1 - me.zl)], n0, n1, n2, n3)
    gd = WeightScatter(me, wires, GD, 0, HID, w0, w1)
    gus = [WeightScatter(me, wires, GU, i * 128, 128, v0, v1) for i in range(4)]

    t.start_z()
    u.start_y()
    t.start(0)
    gain_copies = [wires.start(gain, gains.at[me.f], where) for where in me.x_peers + [me.other_core]]
    here = [
        pltpu.make_async_copy(src, dst, local.at[i])
        for i, (src, dst) in enumerate(
            [
                (tok, T.at[me.f, t.rows(0)]),
                (gain, gains.at[me.f]),
                (up_own, U.at[me.s]),
                (taps_all.at[:, quarter], taps),
                (gout, G.at[me.f, g.rows(0)]),
                (down_own, D.at[me.s]),
            ]
        )
    ]
    for copy in here:
        copy.start()
    u.start_z()
    g.start(0)
    field[...] = jnp.zeros_like(field)
    d_field[...] = jnp.zeros_like(d_field)
    t.forward(0)
    t.start(1)
    g.start_z()
    for copy in gain_copies[:3]:
        copy.wait_recv()
    for k in (1, 2, 3):
        block = gains.at[me.feat(k)]
        gain_copies.append(wires.start(block, block, me.other_core))
    u.forward_own()
    t.finish(0)
    g.forward(0)
    t.forward(1)
    u.start_other()
    d.start_z()
    g.start(1)
    t.finish(1)
    d.start_y()
    g.start(2)
    for copy in here:
        copy.wait()
    for copy in gain_copies[3:]:
        copy.wait_recv()
    t.wait_cores()

    def normalise(r):
        rows = chunk(r)
        squares = jnp.zeros((CHUNK, 128), jnp.float32)
        for k in range(8):
            for lane in range(0, B, 128):
                value = T[k, rows, pl.ds(lane, 128)].astype(jnp.float32)
                squares = squares + value * value
        mean = jnp.sum(squares, axis=1, keepdims=True) / 4096.0
        inv = jnp.broadcast_to(lax.rsqrt(mean + epsilon), (CHUNK, 128))
        inverse[rows, :] = inv
        for k in range(8):
            for lane in range(0, B, 128):
                lanes = pl.ds(lane, 128)
                value = T[k, rows, lanes].astype(jnp.float32) * inv * gains[k, 0:1, lanes]
                N[k, rows, lanes] = value.astype(jnp.bfloat16)

    loop(8, normalise)
    total[...] = jnp.zeros_like(total)

    def lift(zh):
        def body(i):
            j = zh * 4 + i
            for half in range(2):
                total[pl.ds(half * B, B), :] += dot(N[j], U[j, :, pl.ds(half * HID, HID)], 1, 0)

        loop(4, body)

    u.wait_far()
    g.finish(0)
    g.forward(1)
    lift(me.zh)
    u.forward_other()
    d.forward_own()
    g.start(3)
    d.start_other()
    g.finish(1)
    g.forward(2)
    u.wait_far_other()
    lift(1 - me.zh)

    def round_lift(r):
        lift_here[chunk(r), :] = total[chunk(r), :].astype(jnp.bfloat16)

    loop(16, round_lift)
    lift_side = lambda zh: lift_here.at[pl.ds(pl.multiple_of(zh * B, B), B)]
    lift_copy = wires.start(lift_side(1 - me.zh), lift_came, me.other_zh)
    g.forward(3)
    d.wait_far()
    d.forward_other()
    g.finish(2)
    mine = lift_side(me.zh)
    for snap in range(2):
        put_rows(snap * 2 + me.zh, lambda p: mine[pl.ds(snap * 256 + p * CHUNK, CHUNK), :], field, planes.at[0])
    lift_copy.wait_recv()
    for snap in range(2):
        put_rows(
            snap * 2 + 1 - me.zh, lambda p: lift_came[pl.ds(snap * 256 + p * CHUNK, CHUNK), :], field, planes.at[0]
        )
    halo = Halo(me, wires, planes.at[0], came.at[0], field)
    halo.start()

    def activate(rows, lanes, preact):
        value, rate = gelu_pair(preact)
        active[rows, lanes] = value.astype(jnp.bfloat16)
        slope[rows, lanes] = rate

    conv_planes(field, taps, False, 8, inner, activate)
    halo.wait()
    conv_planes(field, taps, False, 8, outer, activate)
    d.wait_far_other()

    def branch_term(j):
        PB[j] = dot(active[...], D[j], 1, 0).astype(jnp.bfloat16)

    loop(8, branch_term)
    b.start_core()
    g.finish(3)
    g.wait_cores()
    gathered = len(wires.copies)
    total[...] = jnp.zeros_like(total)

    def d_active(j):
        total[...] += dot(G[j], D[j], 1, 1)

    loop(8, d_active)

    def d_preact(i):
        part = i
        put_rows(
            part,
            lambda p: total[chunk(part * 4 + p), :] * slope[chunk(part * 4 + p), :],
            d_field,
            planes.at[1],
        )

    loop(4, d_preact)
    d_halo = Halo(me, wires, planes.at[1], came.at[1], d_field)
    d_halo.start()

    b.start_far()
    wires.flush(gathered)

    def down_term(j):
        GD[j, pl.ds(0, HID), :] = dot(active[...], G[j], 0, 0).astype(jnp.bfloat16)

    loop(8, down_term)
    gd.start_far()
    gd.start_direct()

    def d_lift(rows, lanes, value):
        d_slabs[rows, lanes] = value.astype(jnp.bfloat16)

    conv_planes(d_field, taps, True, 8, inner, d_lift)
    d_halo.wait()
    conv_planes(d_field, taps, True, 8, outer, d_lift)
    d_columns = pl.ds(pl.multiple_of(me.zh * HID, HID), HID)
    d_copies = [
        wires.start(
            d_slabs.at[pl.ds(pl.multiple_of((snap * 2 + 1 - me.zh) * 256, 256), 256), :],
            d_lifted.at[pl.ds(snap * 256, 256), d_columns],
            me.other_zh,
        )
        for snap in range(2)
    ]
    gd.start_near()
    for snap in range(2):
        d_lifted[pl.ds(snap * 256, 256), d_columns] = d_slabs[
            pl.ds(pl.multiple_of((snap * 2 + me.zh) * 256, 256), 256), :
        ]
    for copy in d_copies:
        copy.wait_recv()
    b.start_near()

    def up_term(j):
        GU[j, pl.ds(0, B), :] = dot(N[j], d_lifted[...], 0, 0).astype(jnp.bfloat16)

    loop(8, up_term)
    for part in gus:
        part.start_far()
    gd.start_quarters(down_out.at[quarter, :], local.at[0])

    def norm_term(j):
        PN[j] = dot(d_lifted[...], U[j], 1, 1).astype(jnp.bfloat16)

    loop(8, norm_term)
    n.start_core()
    n.start_far()

    conv_sums[...] = jnp.zeros_like(conv_sums)

    def taps_grad(i):
        part, p = lax.div(i, 4), lax.rem(i, 4)
        for lane in range(0, HID, 128):
            lanes = pl.ds(lane, 128)
            here_d = d_field[part * 6 + 1 + p, pl.ds(1, 8), :, lanes]
            by_c = [shift(here_d, -1), here_d, shift(here_d, 1)]
            for a in range(3):
                for b_ in range(3):
                    window = field[part * 6 + p + a, pl.ds(b_, 8), :, lanes]
                    for c in range(3):
                        term = jnp.sum(by_c[c] * window, axis=0)
                        conv_sums[a * 9 + b_ * 3 + c, :, lanes] += term

    loop(16, taps_grad)
    conv_terms[me.y] = jnp.sum(conv_sums[...], axis=1).astype(jnp.bfloat16)
    conv_copies = [wires.start(conv_terms.at[me.y], conv_terms.at[me.y], where) for where in me.y_peers]

    b.start_z()
    for part in gus[:2]:
        part.start_direct()
        part.start_near()
    n.start_near()
    for copy in conv_copies:
        copy.wait_recv()
    conv = conv_terms[0].astype(jnp.float32)
    for k in range(1, 4):
        conv = conv + conv_terms[k].astype(jnp.float32)
    conv_here = conv_out.at[:, quarter]
    conv_here[...] = conv
    last_copies = [wires.start(conv_here, conv_here, where) for where, _ in me.z_peers]
    gus[0].start_z(v2)
    gus[2].start_direct()
    gus[2].start_near()
    n.start_z()
    gus[1].start_z(v2)
    gus[3].start_direct()
    gus[3].start_near()
    up_rows = lambda i: up_out.at[pl.ds(i * 128, 128), hidden]
    gus[0].start_out(up_rows(0), local.at[1])
    gus[2].start_z(v2)
    n.wait()

    def rows_part(r, gain_sum):
        rows = chunk(r)
        whole = n.result(rows)
        d_norm[rows, :] = whole
        inv = inverse[chunk(r, me.zl * 256), :]
        part = jnp.zeros((CHUNK, 128), jnp.float32)
        sums = []
        for lane in range(0, B, 128):
            lanes = slice(lane, lane + 128)
            with_hat = whole[:, lanes] * (tok[rows, lanes].astype(jnp.float32) * inv)
            part = part + with_hat * gain[0:1, lanes]
            sums.append(jnp.sum(with_hat.reshape(8, 8, 128), axis=0))
        row_part[rows, :] = part
        return gain_sum + jnp.concatenate(sums, axis=1)

    gain_sum = lax.fori_loop(0, 4, rows_part, jnp.zeros((8, B), jnp.float32))
    row_sum = jnp.sum(jnp.transpose(row_part[...]), axis=0, keepdims=True)
    row_pair[me.c] = jnp.broadcast_to(row_sum, (8, 256))
    row_copy = wires.start(row_pair.at[me.c], row_pair.at[me.c], me.other_core)
    gain_z[me.rb] = jnp.broadcast_to(jnp.sum(gain_sum, axis=0, keepdims=True), (8, B))
    gain_copies = [wires.start(gain_z.at[me.rb], gain_z.at[me.rb], where) for where, _ in me.z_peers]
    row_copy.wait_recv()
    row_terms[me.x] = row_pair[0] + row_pair[1]
    row_copies = [wires.start(row_terms.at[me.x], row_terms.at[me.x], where) for where in me.x_peers]
    gus[3].start_z(v2)
    gus[1].start_out(up_rows(1), local.at[2])
    gus[2].start_out(up_rows(2), local.at[3])
    for copy in gain_copies:
        copy.wait_recv()
    gain_terms[me.y] = (gain_z[0] + gain_z[1]) + (gain_z[2] + gain_z[3])
    last_copies += [wires.start(gain_terms.at[me.y], gain_terms.at[me.y], where) for where in me.y_peers]
    for copy in row_copies:
        copy.wait_recv()
    rows_sum = (row_terms[0] + row_terms[1]) + (row_terms[2] + row_terms[3])
    row_part[...] = jnp.transpose(jnp.broadcast_to(rows_sum[0:1, :], (128, 256)))
    gus[3].start_out(up_rows(3), local.at[4])

    def finish(r):
        rows = chunk(r)
        inv = inverse[chunk(r, me.zl * 256), :]
        share = row_part[rows, :] / 4096.0
        for lane in range(0, B, 128):
            lanes = slice(lane, lane + 128)
            hat = tok[rows, lanes].astype(jnp.float32) * inv
            value = inv * (d_norm[rows, lanes] * gain[0:1, lanes] - hat * share)
            tokens_out[rows, lanes] = (gout[rows, lanes].astype(jnp.float32) + value).astype(jnp.bfloat16)

    loop(4, finish)
    b.wait()

    def mix(r):
        rows = chunk(r)
        mixed_out[rows, :] = (tok[rows, :].astype(jnp.float32) + b.result(rows)).astype(jnp.bfloat16)

    loop(4, mix)
    for copy in last_copies:
        copy.wait_recv()
    gain_out[...] = ((gain_terms[0] + gain_terms[1]) + (gain_terms[2] + gain_terms[3]))[0:1, :]
    for part in [gd] + gus:
        part.wait_out()
    wires.flush()


def block(tok, gout, gain, up, down, taps):
    vmem = pl.BlockSpec(memory_space=pltpu.VMEM)
    anywhere = pl.BlockSpec(memory_space=pl.ANY)
    bf16, f32 = jnp.bfloat16, jnp.float32
    blocks = lambda *shape: pltpu.VMEM(shape, bf16)
    floats = lambda *shape: pltpu.VMEM(shape, f32)
    return pl.pallas_call(
        block_kernel,
        out_shape=[
            jax.ShapeDtypeStruct((256, B), bf16),
            jax.ShapeDtypeStruct((256, B), bf16),
            jax.ShapeDtypeStruct((B, 2 * B), bf16),
            jax.ShapeDtypeStruct((2 * B, B), bf16),
            jax.ShapeDtypeStruct((32, 2 * B), f32),
            jax.ShapeDtypeStruct((1, B), f32),
        ],
        in_specs=[vmem, vmem, vmem, anywhere, anywhere, anywhere],
        out_specs=[vmem, vmem, anywhere, anywhere, vmem, vmem],
        scratch_shapes=[
            blocks(8, B, B),
            blocks(8, 2 * B, B),
            blocks(8, B, B),
            blocks(8, HID, B),
            blocks(8, B, B),
            blocks(8, 2 * B, B),
            floats(8, 1, B),
            floats(27, HID),
            floats(24, 10, 8, HID),
            floats(24, 10, 8, HID),
            floats(2 * B, HID),
            floats(2 * B, HID),
            blocks(2 * B, HID),
            blocks(B, B),
            floats(B, 128),
            blocks(2 * B, HID),
            blocks(B, HID),
            blocks(2, 2, 4, CHUNK, HID),
            blocks(2, 2, 4, CHUNK, HID),
            floats(256, B),
            floats(256, 128),
            floats(32, 8, HID),
            blocks(4, 32, HID),
            floats(2, 8, 256),
            floats(4, 8, 256),
            floats(4, 8, B),
            floats(4, 8, B),
        ]
        + RowScatter.scratch(2 * B, 3)
        + RowScatter.scratch(B, 1)
        + WeightScatter.scratch(HID)
        + WeightScatter.scratch(B)
        + [blocks(B, B)]
        + [pltpu.SemaphoreType.DMA((6,)), pltpu.SemaphoreType.DMA((200,)), pltpu.SemaphoreType.DMA((200,))],
        compiler_params=pltpu.CompilerParams(
            collective_id=0, has_side_effects=True, vmem_limit_bytes=62 << 20
        ),
        name="block",
    )(tok, gout, gain, up, down, taps)


def place_kernel(*refs):
    count = len(refs) // 3
    ins, outs, held, cut, sems = refs[:count], refs[count : 2 * count], refs[2 * count : -2], refs[-2], refs[-1]
    arriving = [pltpu.make_async_copy(src, mid, sems.at[0, i]) for i, (src, mid) in enumerate(zip(ins, held))]
    for copy in arriving:
        copy.start()
    leaving = []
    for i, (mid, dst) in enumerate(zip(held, outs)):
        arriving[i].wait()
        src = mid
        if mid.shape != dst.shape:
            cut[...] = mid[: dst.shape[0], :]
            src = cut
        leaving.append(pltpu.make_async_copy(src, dst, sems.at[1, i]))
        leaving[-1].start()
    for copy in leaving:
        copy.wait()


def place(arrays, rows):
    shapes = [(rows,) + a.shape[1:] if i == 4 else a.shape for i, a in enumerate(arrays)]
    specs = [pl.BlockSpec(memory_space=pl.ANY)] * len(arrays)
    return pl.pallas_call(
        place_kernel,
        out_shape=[jax.ShapeDtypeStruct(shape, a.dtype) for shape, a in zip(shapes, arrays)],
        in_specs=specs,
        out_specs=specs,
        scratch_shapes=[pltpu.VMEM(a.shape, a.dtype) for a in arrays]
        + [pltpu.VMEM(shapes[4], jnp.float32), pltpu.SemaphoreType.DMA((2, len(arrays)))],
        name="place",
    )(*arrays)


def per_device(tokens, grad_out, gain, up_weight, down_weight, conv_taps):
    tok = tokens.reshape(256, B)
    gout = grad_out.reshape(256, B)
    outs = block(tok, gout, gain.reshape(1, B), up_weight, down_weight, conv_taps)
    mixed, grad_tokens, grad_up, grad_down, grad_conv, grad_gain = place(outs, conv_taps.shape[0])
    return (
        mixed.reshape(tokens.shape),
        grad_tokens.reshape(tokens.shape),
        grad_up,
        grad_down,
        grad_conv,
        grad_gain.reshape(B),
    )


def solution(mesh):
    rows = P("dp", "seq", None, None, "fsdp")
    return jax.shard_map(
        per_device,
        mesh=mesh,
        in_specs=(rows, rows, P("fsdp"), P("seq", "fsdp"), P("fsdp", "seq"), P(None, "fsdp")),
        out_specs=(rows, rows, P("seq", "fsdp"), P("fsdp", "seq"), P(None, "fsdp"), P("fsdp")),
        check_vma=False,
    )
```
